32 devices in a mesh: pipe: 4 (over y, core), dp: 4 (over z), tensor: 2 (over x).
Axes of the slice: x: 2, y: 2, z: 4, core: 2. Of those that a mesh axis runs over, the one named last changes fastest.
Arguments:
- output_gradient: bfloat16 [16, 128, 8192], P('dp', None, 'tensor'), may hold values from -6 to 6
- acts: bfloat16 [16, 4, 128, 8192], P('dp', 'pipe', None, 'tensor'), may hold values from -6 to 6
- weights: bfloat16 [4, 8192, 8192], P('pipe', 'tensor'), may hold values from -0.0625 to 0.0625
- adapter_down_factors: bfloat16 [4, 8192, 128], P('pipe', 'tensor'), may hold values from -0.0625 to 0.0625
- adapter_up_factors: bfloat16 [4, 128, 8192], P('pipe'), may hold values from -0.0625 to 0.0625
- feature_sign_bits: int32 [8192, 64], replicated, may hold values from 0 to 1
- rank_sign_bits: int32 [128, 128], replicated, may hold values from 0 to 1
- lengths: int32 [16], P('dp'), may hold values from 32 to 128, as said below
Outputs:
- features: float32 [16, 4, 8192], P('dp', 'pipe', 'tensor')
The draws below stay inside these ranges and needn't reach their ends.
Inputs may be any that keep to these rules, and one draw needn't show every extreme that they name: `lengths`: the first example has exactly 128 real tokens.
All inputs are finite; a program needn't handle non-finite values.
Results may differ from the reference program's by a relative error of at most 0.0065.
Values may be sent and summed in bfloat16 or wider, within the bound.
No kernel may reach another device: no remote copies, remote signals or barrier semaphores. Data moves between devices by JAX's collectives and lax.ppermute only.
A program may use at most 192 MiB of HBM per device.

```python
import math
import jax
import jax.numpy as jnp
from jax import lax

MODEL_WIDTH = 8192
ADAPTER_RANK = 128
PROJ = 64
LEN = 128
SECTION_COUNT = 4
EXAMPLES = 16


def draw_lengths(key, part):
    values = jax.random.randint(key, (EXAMPLES,), LEN // 4, LEN + 1)
    return values.at[0].set(LEN).astype(jnp.int32)


def with_ends(entries, rng, low, largest):
    place = [jax.random.randint(jax.random.fold_in(rng, axis), (), 0, length) for axis, length in enumerate(entries.shape)]
    longest = entries.shape.index(max(entries.shape))
    neighbour = place[:longest] + [(place[longest] + 1) % entries.shape[longest]] + place[longest + 1:]
    return entries.at[tuple(place)].set(low).at[tuple(neighbour)].set(largest)


def steps_of(key, shape, pieces, least, largest):
    level = 1.0
    for position, blocks in pieces:
        heights = jax.random.uniform(jax.random.fold_in(jax.random.fold_in(key, 6), position), (blocks,), jnp.float32, least / len(pieces), largest / len(pieces))
        level = level * jnp.repeat(jnp.exp(heights), shape[position] // blocks).reshape((-1,) + (1,) * (len(shape) - 1 - position))
    return level


def noise(stream_key, shape, deviation, reach, split=(), held_as=jnp.bfloat16):
    gain = steps_of(stream_key, shape, split, -0.22, 0.18) if split else 1.0
    drawn = jax.random.normal(stream_key, shape, jnp.float32) * deviation * gain
    return jnp.minimum(jnp.maximum(drawn, -reach), reach).astype(held_as)


def setup_inputs(seed: int = 0) -> dict:
    key_list = jax.random.split(jax.random.key(seed), 9)
    output_gradient = noise(key_list[0], (EXAMPLES, LEN, MODEL_WIDTH), 1.0, 6.0, ((0, 4), (2, 2)))
    acts = noise(key_list[1], (EXAMPLES, SECTION_COUNT, LEN, MODEL_WIDTH), 1.0, 6.0, ((0, 4), (1, 4), (3, 2)))
    weights = noise(key_list[2], (SECTION_COUNT, MODEL_WIDTH, MODEL_WIDTH), MODEL_WIDTH ** -0.5, 0.0625, ((0, 4), (1, 2)))
    adapter_down_factors = noise(key_list[3], (SECTION_COUNT, MODEL_WIDTH, ADAPTER_RANK), MODEL_WIDTH ** -0.5, 0.0625, ((0, 4), (1, 2)))
    adapter_up_factors = noise(key_list[4], (SECTION_COUNT, ADAPTER_RANK, MODEL_WIDTH), MODEL_WIDTH ** -0.5, 0.0625, ((0, 4),))
    feature_sign_bits = with_ends(jax.random.randint(key_list[5], (MODEL_WIDTH, PROJ), 0, 2), jax.random.fold_in(key_list[5], 1), 0, 1).astype(jnp.int32)
    rank_sign_bits = with_ends(jax.random.randint(key_list[6], (ADAPTER_RANK, 2 * PROJ), 0, 2), jax.random.fold_in(key_list[6], 1), 0, 1).astype(jnp.int32)
    lengths = draw_lengths(jax.random.fold_in(key_list[8], 71), 0)
    return {"output_gradient": output_gradient, "acts": acts, "weights": weights, "adapter_down_factors": adapter_down_factors, "adapter_up_factors": adapter_up_factors, "feature_sign_bits": feature_sign_bits, "rank_sign_bits": rank_sign_bits, "lengths": lengths}


ADAPTER_SCALE = 2.0

def features_of(xp, xb, uq, yp, keep, seq):
    xp = xp * keep[:, None]
    xb = xb * keep[:, None]
    left = jnp.dot(xp.T, uq, precision=lax.Precision.HIGHEST, preferred_element_type=jnp.float32)
    right = jnp.dot(xb.T, yp.astype(jnp.float32), precision=lax.Precision.HIGHEST, preferred_element_type=jnp.float32)
    return jnp.concatenate([left.reshape(-1), right.reshape(-1)]) * (ADAPTER_SCALE / math.sqrt(seq))

def reference(output_gradient, acts, weights, adapter_down_factors, adapter_up_factors, feature_sign_bits, rank_sign_bits, lengths):
    wide = (2 * feature_sign_bits - 1).astype(jnp.bfloat16)
    low = (2 * rank_sign_bits - 1).astype(jnp.float32)
    low_left = low[:, :PROJ].astype(jnp.bfloat16)
    low_right = low[:, PROJ:]
    inv_d = 1.0 / math.sqrt(MODEL_WIDTH)
    inv_r = 1.0 / math.sqrt(ADAPTER_RANK)
    positions = jnp.arange(LEN)

    def one_example(items):
        running_gradient, inputs, length = items
        keep = (positions < length).astype(jnp.float32)
        results = []
        for section_index in reversed(range(SECTION_COUNT)):
            current_input = inputs[section_index]
            update_gradient = jnp.dot(running_gradient, adapter_up_factors[section_index].T, preferred_element_type=jnp.float32).astype(jnp.bfloat16)
            y_proj = (jnp.dot(running_gradient, wide, preferred_element_type=jnp.float32) * inv_d).astype(jnp.bfloat16)
            x_proj = jnp.dot(current_input, wide, preferred_element_type=jnp.float32) * inv_d
            input_down_projected = jnp.dot(current_input, adapter_down_factors[section_index], preferred_element_type=jnp.float32)
            u_proj = jnp.dot(update_gradient, low_left, preferred_element_type=jnp.float32) * inv_r
            x_low = jnp.dot(input_down_projected, low_right, precision=lax.Precision.HIGHEST, preferred_element_type=jnp.float32) * inv_r
            results.append(features_of(x_proj, x_low, u_proj, y_proj, keep, LEN))
            frozen_weight = jnp.dot(running_gradient, weights[section_index].T, preferred_element_type=jnp.float32)
            running_gradient = (frozen_weight + ADAPTER_SCALE * jnp.dot(update_gradient, adapter_down_factors[section_index].T, preferred_element_type=jnp.float32)).astype(jnp.bfloat16)
        return jnp.stack(results[::-1])
    return lax.map(one_example, (output_gradient, acts, lengths))
```

```python
import functools
import math

import jax
import jax.numpy as jnp
from jax import lax
from jax.experimental import pallas as pl
from jax.experimental.pallas import tpu as pltpu
from jax.sharding import PartitionSpec as P

ADAPTER_SCALE = 2.0
AXES = ("pipe", "dp", "tensor")
F32 = jnp.float32
BF16 = jnp.bfloat16


def nt(left, right, precision=None):
    return lax.dot_general(
        left, right, (((1,), (1,)), ((), ())), precision=precision, preferred_element_type=F32
    )


def shift(value, source_stage, target_stage, by_dp, by_tensor):
    groups, parts = lax.axis_size("dp"), lax.axis_size("tensor")

    def place(stage, group, part):
        return (stage * groups + group % groups) * parts + part % parts

    pairs = [
        (place(source_stage, g, k), place(target_stage, g + by_dp, k + by_tensor))
        for g in range(groups)
        for k in range(parts)
    ]
    return lax.ppermute(value, AXES, pairs)


def pull_kernel(group, x_ref, w_ref, a_ref, b_ref, out_ref, low_ref):
    @pl.when(pl.program_id(0) == 0)
    def _():
        low = jnp.dot(x_ref[...], a_ref[...], preferred_element_type=F32)
        low_ref[...] = (ADAPTER_SCALE * low).astype(BF16)

    total = jnp.dot(x_ref[...], w_ref[...], preferred_element_type=F32)
    total += jnp.dot(low_ref[...], b_ref[...], preferred_element_type=F32)
    out_ref[...] = total.astype(BF16)


def pull(x, weight, down, up, group, groups, parts):
    rows, depth = x.shape
    rank, width = up.shape
    run = width // parts // groups
    block = min(512, run)
    per_run = run // block

    def column(j, group_ref):
        return (j // per_run) * (groups * per_run) + group_ref[0] * per_run + j % per_run

    return pl.pallas_call(
        pull_kernel,
        grid_spec=pltpu.PrefetchScalarGridSpec(
            num_scalar_prefetch=1,
            grid=(parts * per_run,),
            in_specs=[
                pl.BlockSpec((rows, depth), lambda j, g: (0, 0)),
                pl.BlockSpec((depth, block), lambda j, g: (0, column(j, g))),
                pl.BlockSpec((depth, rank), lambda j, g: (0, 0)),
                pl.BlockSpec((rank, block), lambda j, g: (0, column(j, g))),
            ],
            out_specs=pl.BlockSpec((rows, block), lambda j, g: (0, j)),
            scratch_shapes=[pltpu.VMEM((rows, rank), BF16)],
        ),
        out_shape=jax.ShapeDtypeStruct((rows, parts * run), BF16),
        compiler_params=pltpu.CompilerParams(vmem_limit_bytes=40 * 2**20),
    )(group.reshape(1), x, weight, down, up)


def first_push_kernel(part, g_ref, w_ref, out_ref):
    out_ref[...] = nt(g_ref[...], w_ref[...])


def first_push(grad, weight, part):
    tokens, depth = grad.shape
    rows = weight.shape[0]
    block = min(512, rows)
    return pl.pallas_call(
        first_push_kernel,
        grid_spec=pltpu.PrefetchScalarGridSpec(
            num_scalar_prefetch=1,
            grid=(rows // block,),
            in_specs=[
                pl.BlockSpec((tokens, depth), lambda i, p: (0, 0)),
                pl.BlockSpec((block, depth), lambda i, p: (i, p[0])),
            ],
            out_specs=pl.BlockSpec((tokens, block), lambda i, p: (0, i)),
        ),
        out_shape=jax.ShapeDtypeStruct((tokens, rows), F32),
        compiler_params=pltpu.CompilerParams(vmem_limit_bytes=40 * 2**20),
    )(part.reshape(1), grad, weight)


def last_push_kernel(others, part, near_ref, far_ref, w_ref, acc_ref, u_ref, a_ref, out_ref, total_ref):
    k = pl.program_id(1)

    @pl.when(k == 0)
    def _():
        total_ref[...] = acc_ref[...] + ADAPTER_SCALE * nt(u_ref[...], a_ref[...])

    half = near_ref.shape[1]
    total_ref[:half] += nt(near_ref[0], w_ref[...])
    total_ref[half:] += nt(far_ref[0], w_ref[...])

    @pl.when(k == others - 1)
    def _():
        out_ref[...] = total_ref[...].astype(BF16)


def last_push(near, far, weight, total, u_all, down, part, parts):
    others, half, depth = near.shape
    tokens = total.shape[0]
    rows = weight.shape[0]
    rank = down.shape[1]
    block = min(512, rows)
    return pl.pallas_call(
        functools.partial(last_push_kernel, others),
        grid_spec=pltpu.PrefetchScalarGridSpec(
            num_scalar_prefetch=1,
            grid=(rows // block, others),
            in_specs=[
                pl.BlockSpec((1, half, depth), lambda i, k, p: (k, 0, 0)),
                pl.BlockSpec((1, half, depth), lambda i, k, p: (k, 0, 0)),
                pl.BlockSpec((block, depth), lambda i, k, p: (i, lax.rem(p[0] + k + 1, parts))),
                pl.BlockSpec((tokens, block), lambda i, k, p: (0, i)),
                pl.BlockSpec((tokens, rank), lambda i, k, p: (0, 0)),
                pl.BlockSpec((block, rank), lambda i, k, p: (i, 0)),
            ],
            out_specs=pl.BlockSpec((tokens, block), lambda i, k, p: (0, i)),
            scratch_shapes=[pltpu.VMEM((tokens, block), F32)],
        ),
        out_shape=jax.ShapeDtypeStruct((tokens, rows), BF16),
        compiler_params=pltpu.CompilerParams(vmem_limit_bytes=40 * 2**20),
    )(part.reshape(1), near, far, weight, total, u_all, down)


def per_device(
    output_gradient,
    acts,
    weights,
    adapter_down_factors,
    adapter_up_factors,
    feature_sign_bits,
    rank_sign_bits,
    lengths,
):
    stages, groups, parts = (lax.axis_size(name) for name in AXES)
    stage, group, part = (lax.axis_index(name) for name in AXES)
    last = stages - 1
    count, seq, local = output_gradient.shape
    tokens = count * seq
    width = local * parts
    rank = adapter_up_factors.shape[1]
    proj = feature_sign_bits.shape[1]
    run = local // groups
    grad = output_gradient.reshape(tokens, local)
    saved = acts[:, 0].reshape(tokens, local)
    weight, down, up = weights[0], adapter_down_factors[0], adapter_up_factors[0]

    def local_columns(whole, which):
        return lax.dynamic_slice_in_dim(whole, which * local, local, 1)

    near = [shift(grad[: tokens // 2], last, last, 0, -k) for k in range(1, parts)]
    far = [shift(grad[tokens // 2 :], 0, last, 0, -k) for k in range(1, parts)]

    bits = lax.dynamic_slice_in_dim(feature_sign_bits, part * local, local, 0)
    signs = (2 * bits - 1).astype(BF16).T
    low = 2 * rank_sign_bits - 1
    low_left, low_right = low[:, :proj].astype(BF16), low[:, proj:].astype(F32)

    up_low = lax.dot_general(
        low_left, local_columns(up, part), (((0,), (0,)), ((), ())), preferred_element_type=F32
    ).astype(BF16)
    below = [shift(up_low, s, s + 1, 0, 0) for s in range(last)]

    def on(wanted, step, shape, dtype):
        return lax.cond(stage == wanted, step, lambda: jnp.zeros(shape, dtype))

    reach = {last - 1: []}
    moving = None
    finished = []
    for s in range(1, last):
        own = jnp.concatenate([below[s - 1], signs])
        if s > 1:
            whole = on(
                s, lambda: pull(own, weight, down, up, 0 * group, 1, parts), (2 * proj, width), BF16
            )
            total = 0
            for k in range(parts):
                target = lax.rem(part + k, parts)
                total += shift(local_columns(whole, target), s, s + 1, 0, k).astype(F32)
            finished.append(total.astype(BF16))
        source = own if s == 1 else moving
        pulled = on(
            s,
            lambda: pull(source, weight, down, up, group, groups, parts),
            (2 * proj, parts * run),
            BF16,
        )
        total = 0
        for k in range(parts):
            target = lax.rem(part + k, parts)
            total += shift(lax.dynamic_slice_in_dim(pulled, target * run, run, 1), s, s + 1, 0, k).astype(F32)
        slice_ = total.astype(BF16)
        moving = jnp.zeros((2 * proj, local), BF16)
        moving = lax.dynamic_update_slice_in_dim(moving, slice_, group * run, 1)
        for k in range(1, groups):
            origin = lax.rem(group + groups - k, groups)
            arrived = shift(slice_, s + 1, s + 1, k, 0)
            moving = lax.dynamic_update_slice_in_dim(moving, arrived, origin * run, 1)

    begun = on(last, lambda: first_push(grad, weight, part), (tokens, local), F32)
    near, far = jnp.stack(near), jnp.stack(far)

    def finish():
        def sums(right):
            total = nt(grad, right[0])
            for k in range(1, parts):
                other = jnp.concatenate([near[k - 1], far[k - 1]])
                total += nt(other, right[k])
            return total

        order = [lax.rem(part + k, parts) for k in range(parts)]
        u_all = sums([local_columns(up, q) for q in order]).astype(BF16)
        every = (2 * feature_sign_bits - 1).astype(BF16).T
        yp = sums([local_columns(every, q) for q in order])
        uq = jnp.dot(u_all, low_left, preferred_element_type=F32)
        return last_push(near, far, weight, begun, u_all, down, part, parts), jnp.concatenate([uq, yp], 1)

    grad_below, mine_last = lax.cond(
        stage == last,
        finish,
        lambda: (jnp.zeros((tokens, local), BF16), jnp.zeros((tokens, 2 * proj), F32)),
    )

    x_signs = nt(saved, signs)
    x_down = jnp.dot(saved, down, preferred_element_type=F32)
    x_low = jnp.dot(x_down, low_right, precision=lax.Precision.HIGHEST, preferred_element_type=F32)
    x_part = jnp.concatenate([x_signs, x_low], 1)
    share = 2 * proj // parts
    x_side = 0
    for k in range(parts):
        target = lax.rem(part + k, parts)
        piece = lax.dynamic_slice_in_dim(x_part, target * share, share, 1)
        if k:
            piece = lax.ppermute(piece, "tensor", [(q, (q + k) % parts) for q in range(parts)])
        x_side += piece

    def side_of(which):
        return which * 2 // parts * proj

    y_side = lax.dynamic_slice_in_dim(mine_last, side_of(part), proj, 1)
    rights = [jnp.concatenate([below[last - 1], signs])] + finished + [moving]
    for s, right in zip(range(last - 1, -1, -1), rights):
        y_part = nt(grad_below, right)
        total = 0
        for k in range(parts):
            target = lax.rem(part + k, parts)
            piece = lax.dynamic_slice_in_dim(y_part, side_of(target), proj, 1)
            total += shift(piece, last, s, 0, k)
        y_side = jnp.where(stage == s, total, y_side)

    keep = jnp.arange(seq)[None, :] < lengths[:, None]
    scale = ADAPTER_SCALE / math.sqrt(seq) / math.sqrt(width) / math.sqrt(rank)
    left = jnp.where(keep[:, :, None], x_side.reshape(count, seq, share), 0.0) * scale
    right = y_side.reshape(count, seq, proj)
    feats = lax.dot_general(
        left,
        right,
        (((1,), (1,)), ((0,), (0,))),
        precision=lax.Precision.HIGHEST,
        preferred_element_type=F32,
    )
    return feats.reshape(count, 1, share * proj)


def solution(mesh):
    placed = (
        P("dp", None, "tensor"),
        P("dp", "pipe", None, "tensor"),
        P("pipe", "tensor", None),
        P("pipe", "tensor", None),
        P("pipe", None, None),
        P(),
        P(),
        P("dp"),
    )
    return jax.shard_map(
        per_device, mesh=mesh, in_specs=placed, out_specs=P("dp", "pipe", "tensor"), check_vma=False
    )
```

```python
import math

import jax
import jax.numpy as jnp
from jax import lax
from jax.experimental import pallas as pl
from jax.experimental.pallas import tpu as pltpu
from jax.sharding import PartitionSpec as P

ADAPTER_SCALE = 2.0
AXES = ("pipe", "dp", "tensor")
F32 = jnp.float32
BF16 = jnp.bfloat16
SMEM, VMEM, HBM, ANY = pltpu.SMEM, pltpu.VMEM, pltpu.HBM, pl.ANY
ROWS = 16
BEST = lax.Precision.HIGHEST


def nt(left, right, precision=None):
    return lax.dot_general(
        left, right, (((1,), (1,)), ((), ())), precision=precision, preferred_element_type=F32
    )


def nn(left, right, precision=None):
    return jnp.dot(left, right, precision=precision, preferred_element_type=F32)


def placed(array, space):
    return pltpu.with_memory_space_constraint(array, HBM) if space is HBM else array


def launch(body, ins, outs, scratch=(), after=(), room=22):
    count, extra = len(ins), len(after)

    def kernel(*refs):
        body(*refs[:count], *refs[count + extra :])

    return pl.pallas_call(
        kernel,
        in_specs=[pl.BlockSpec(memory_space=space) for _, space in ins]
        + [pl.BlockSpec(memory_space=ANY)] * extra,
        out_specs=[pl.BlockSpec(memory_space=space) for _, _, space in outs],
        out_shape=[
            pltpu.HBM(shape, dtype) if space is HBM else jax.ShapeDtypeStruct(shape, dtype)
            for shape, dtype, space in outs
        ],
        scratch_shapes=list(scratch),
        compiler_params=pltpu.CompilerParams(vmem_limit_bytes=room * 2**20),
        cost_estimate=pl.CostEstimate(flops=0, bytes_accessed=0, transcendentals=0),
    )(*[placed(array, space) for array, space in ins], *after)


def shift(value, routes, to_group, by_tensor):
    groups, parts = lax.axis_size("dp"), lax.axis_size("tensor")

    def place(stage, group, part):
        return (stage * groups + group) * parts + part % parts

    pairs = [
        (place(source, g, k), place(target, to_group(g), k + by_tensor))
        for source, target in routes
        for g in range(groups)
        for k in range(parts)
    ]
    return lax.ppermute(value, AXES, pairs)


def copies(sems, *pairs):
    made = [pltpu.make_async_copy(source, target, sems.at[i]) for i, (source, target) in enumerate(pairs)]
    for copy in made:
        copy.start()
    return made


def finish(made):
    for copy in made:
        copy.wait()


def packed_at(lengths, count):
    starts = [jnp.int32(0)]
    for e in range(count):
        starts.append(starts[-1] + (lengths[e] + ROWS - 1) // ROWS * ROWS)
    return starts


def by_rows(rows, sizes, step):
    least = 0
    for size in sizes:
        pl.when((rows > least) & (rows <= size))(lambda size=size: step(size))
        least = size


def per_device(
    output_gradient,
    acts,
    weights,
    adapter_down_factors,
    adapter_up_factors,
    feature_sign_bits,
    rank_sign_bits,
    lengths,
):
    stages, groups, parts = (lax.axis_size(name) for name in AXES)
    last = stages - 1
    count, seq, local = output_gradient.shape
    tokens = count * seq
    half = tokens // 2
    width = local * parts
    rank = adapter_up_factors.shape[1]
    proj = feature_sign_bits.shape[1]
    share = 2 * proj // parts
    block = min(512, local)
    spans = groups // 2
    span = local // spans
    piece = min(512, span)
    per_span = span // piece
    weight, down, up = weights[0], adapter_down_factors[0], adapter_up_factors[0]
    bits = feature_sign_bits.T
    info = jnp.stack([lax.axis_index(name) for name in AXES]).astype(jnp.int32)

    def target_of(part, k):
        return lax.rem(part + k, parts)

    def origin_of(group, k):
        return lax.rem(lax.rem(group, spans) + spans - k, spans)

    def neighbour(k):
        return lambda g: g // spans * spans + (g + k) % spans

    def further(k):
        return lambda g: (g + k) % groups

    def same(g):
        return g

    def columns(which):
        return pl.ds(pl.multiple_of(which * local, 128), local)

    def side_of(part):
        return part // (parts // 2)

    def signs_of(values):
        return (2 * values - 1).astype(F32)

    def prepare(info, lengths, bits, low_bits, up, grad, signs, up_low, top, bottom, bits_buf, up_buf, raw, sems):
        mine = columns(info[2])
        is_last = info[0] == last
        made = copies(sems, (up.at[:, mine], up_buf), (bits.at[:, mine], bits_buf))
        loads = [pltpu.make_async_copy(grad.at[e], raw.at[e], sems.at[2 + e]) for e in range(count)]

        @pl.when(is_last)
        def _():
            for load in loads:
                load.start()

        low_left = signs_of(low_bits[...]).T[:proj, :].astype(BF16)
        made[0].wait()
        up_low[...] = nn(low_left, up_buf[...]).astype(BF16)
        made[1].wait()
        signs[...] = signs_of(bits_buf[...]).astype(BF16)

        @pl.when(is_last)
        def _():
            starts = packed_at(lengths, count)
            for e in range(count):
                loads[e].wait()
                for j in range(seq // ROWS):
                    row = starts[e] + ROWS * j
                    real = ROWS * j < lengths[e]

                    @pl.when(real & (row < half))
                    def _(e=e, j=j, row=row):
                        top[pl.ds(pl.multiple_of(row, ROWS), ROWS), :] = raw[e, ROWS * j : ROWS * (j + 1), :]

                    @pl.when(real & (row >= half))
                    def _(e=e, j=j, row=row):
                        there = pl.ds(pl.multiple_of(row - half, ROWS), ROWS)
                        bottom[there, :] = raw[e, ROWS * j : ROWS * (j + 1), :]

    near_targets, far_targets = list(range(max(1, parts // 2))), list(range(max(1, parts // 2), parts))
    ahead = 3
    far_count, near_count = len(far_targets) * per_span, len(near_targets) * per_span

    order = far_targets + near_targets

    def fetches(info, weight, buffer, sems, first, end):
        made = []
        for i in range(first, end):
            column = (
                target_of(info[2], order[i // per_span]) * local
                + lax.rem(info[1], spans) * span
                + i % per_span * piece
            )
            where = pl.ds(pl.multiple_of(column, 128), piece)
            slot = (i - first) % buffer.shape[0]
            made.append(pltpu.make_async_copy(weight.at[:, where], buffer.at[slot], sems.at[slot]))
        return made

    def lookups(info, up, up_buf, sems, targets):
        pairs = []
        for i, k in enumerate(targets):
            column = target_of(info[2], k) * local + lax.rem(info[1], spans) * span
            pairs.append((up.at[:, pl.ds(pl.multiple_of(column, 128), span)], up_buf.at[i]))
        return copies(sems, *pairs)

    def in_turn(made, use):
        for copy in made[:ahead]:
            copy.start()
        for i, copy in enumerate(made):
            copy.wait()
            if i + ahead < len(made):
                made[i + ahead].start()
            use(i)

    def first_step(info, weight, down, up, even, signs, *rest):
        outs, (held, x, low, up_buf, sems, up_sems) = rest[:parts], rest[parts:]
        stage, group = info[0], info[1]

        @pl.when(stage == 1)
        def _():
            made = fetches(info, weight, held, sems, 0, far_count + near_count)
            ready = lookups(info, up, up_buf, up_sems, order)
            x[...] = jnp.where(group < spans, even[...], signs[...])
            low[...] = (ADAPTER_SCALE * nn(x[...], down[...])).astype(BF16)

            def use(i):
                if i == 0:
                    finish(ready)
                at = pl.ds(i % per_span * piece, piece)
                total = nn(x[...], held[i % far_count]) + nn(low[...], up_buf[i // per_span, :, at])
                outs[order[i // per_span]][:, at] = total.astype(BF16)

            in_turn(made, use)

        @pl.when(stage == 2)
        def _():
            in_turn(fetches(info, weight, held, sems, 0, far_count), lambda i: None)

    wide = 3 * proj

    def step_out(i, at, total, outs):
        outs[2 * (i // per_span)][:, at] = total[:proj].astype(BF16)
        outs[2 * (i // per_span) + 1][:, at] = total[proj:].astype(BF16)

    def second_far(info, held, down, up, *rest):
        given, rest = rest[: spans * parts + 2], rest[spans * parts + 2 :]
        outs, (x, low, up_buf, up_sems) = rest[: 2 * len(far_targets)], rest[2 * len(far_targets) :]
        group = info[1]

        @pl.when(info[0] == 2)
        def _():
            ready = lookups(info, up, up_buf, up_sems, far_targets)
            for k in range(spans):
                total = given[k * parts][...].astype(F32)
                for value in given[k * parts + 1 : (k + 1) * parts]:
                    total += value[...].astype(F32)
                first = pl.multiple_of(origin_of(group, k) * span, 128)
                x[:proj, pl.ds(first, span)] = total.astype(BF16)
            x[proj : 2 * proj, :] = given[-2][...]
            x[2 * proj :, :] = given[-1][...]
            low[...] = (ADAPTER_SCALE * nn(x[...], down[...])).astype(BF16)
            finish(ready)
            for i in range(len(far_targets) * per_span):
                at = pl.ds(i % per_span * piece, piece)
                step_out(i, at, nn(x[...], held[i]) + nn(low[...], up_buf[i // per_span, :, at]), outs)

    def second_near(info, weight, up, x, low, *rest):
        outs, (w, up_buf, sems, up_sems) = rest[: 2 * len(near_targets)], rest[2 * len(near_targets) :]

        @pl.when(info[0] == 2)
        def _():
            made = fetches(info, weight, w, sems, far_count, far_count + near_count)
            ready = lookups(info, up, up_buf, up_sems, near_targets)

            def use(i):
                if i == 0:
                    finish(ready)
                at = pl.ds(i % per_span * piece, piece)
                step_out(i, at, nn(x[...], w[i]) + nn(low[...], up_buf[i // per_span, :, at]), outs)

            in_turn(made, use)

    def added(values):
        total = values[0].astype(F32)
        for value in values[1:]:
            total += value.astype(F32)
        return total.astype(BF16)

    blocks, ring = local // block, 4

    def stream(weight, ring_buf, sems, count_of, part_of, use):
        def fetch(n):
            i, k = n // count_of, n % count_of
            first = pl.multiple_of(i * block, block)
            slot = lax.rem(n, ring)
            return pltpu.make_async_copy(
                weight.at[pl.ds(first, block), columns(part_of(k))], ring_buf.at[slot], sems.at[slot]
            )

        total_steps = blocks * count_of
        for n in range(min(ring - 1, total_steps)):
            fetch(jnp.int32(n)).start()

        def step(n, _):
            fetch(n).wait()

            @pl.when(n + ring - 1 < total_steps)
            def _():
                fetch(n + ring - 1).start()

            use(n // count_of, n % count_of, lax.rem(n, ring))
            return 0

        return lambda: lax.fori_loop(0, total_steps, step, 0)

    def push_own(info, lengths, top, bottom, weight, up, signs, total, u_part, y_part, both, ring_buf, sems, ring_sems):
        part = info[2]

        @pl.when(info[0] == last)
        def _():
            rows = packed_at(lengths, count)[count]

            def use(i, k, slot):
                at = pl.ds(pl.multiple_of(i * block, block), block)
                total[:half, at] = nt(top[...], ring_buf[slot])

                def sized(size):
                    total[half : half + size, at] = nt(bottom[:size], ring_buf[slot])

                by_rows(rows - half, range(half // 4, half + 1, half // 4), sized)

            made = copies(sems, (up.at[:, columns(part)], both.at[:rank]))
            go = stream(weight, ring_buf, ring_sems, 1, lambda k: part, use)
            both[rank:, :] = signs[...]
            finish(made)
            for i, grad in enumerate((top, bottom)):
                low = nt(grad[...], both[...])
                u_part[i * half : (i + 1) * half], y_part[i * half : (i + 1) * half] = low[:, :rank], low[:, rank:]
            go()

    def push_rest(which):
        def body(info, lengths, bits, low_bits, weight, up, down, total, u_part, y_part, *rest):
            given, rest = rest[: parts - 1], rest[parts - 1 :]
            below, own, bits_buf, both, u_all, so_far, ring_buf, sems, ring_sems = rest
            part = info[2]
            mine = slice(which * half, (which + 1) * half)

            @pl.when(info[0] == last)
            def _():
                rows = packed_at(lengths, count)[count] - which * half

                def use(i, k, slot):
                    at = pl.ds(pl.multiple_of(i * block, block), block)

                    def sized(size):
                        for j in range(parts - 1):

                            @pl.when(k == j)
                            def _(j=j):
                                value = nt(given[j][:size], ring_buf[slot])
                                if j == 0:
                                    value += total[mine.start : mine.start + size, at]
                                    value += ADAPTER_SCALE * nt(u_all[:size], down[at, :])
                                else:
                                    value += so_far[:size]
                                if j == parts - 2:
                                    below[:size, at] = value.astype(BF16)
                                else:
                                    so_far[:size] = value

                    if which:
                        by_rows(rows, range(half // 4, half + 1, half // 4), sized)
                    else:
                        sized(half)

                pairs = []
                for k in range(parts - 1):
                    there = columns(target_of(part, k + 1))
                    pairs += [(up.at[:, there], both.at[k, :rank]), (bits.at[:, there], bits_buf.at[k])]
                made = copies(sems, *pairs)
                go = stream(weight, ring_buf, ring_sems, parts - 1, lambda k: lax.rem(part + k + 1, parts), use)
                finish(made)
                u_sum, y_sum = u_part[mine, :], y_part[mine, :]
                for k in range(parts - 1):
                    both[k, rank:, :] = signs_of(bits_buf[k]).astype(BF16)
                    low = nt(given[k][...], both[k])
                    u_sum += low[:, :rank]
                    y_sum += low[:, rank:]
                u_all[...] = u_sum.astype(BF16)
                low_left = signs_of(low_bits[...]).T[:proj, :].astype(BF16)
                own[:, :proj] = nt(u_all[...], low_left)
                own[:, proj:] = y_sum
                go()

        return body

    def meet(kind, sources, after=()):
        def body(info, top, bottom, *rest):
            given, rest = rest[: len(sources)], rest[len(sources) :]
            outs, (x,) = rest[:parts], rest[parts:]
            group, part = info[1], info[2]

            @pl.when(info[0] == last)
            def _():
                if kind == "here":
                    x[:proj, :], x[proj:, :] = given[0][...], given[1][...]
                elif kind == "spans":
                    for k in range(spans):
                        x[:, pl.ds(pl.multiple_of(origin_of(group, k) * span, 128), span)] = given[k][...]
                else:
                    for k in range(groups):
                        origin = lax.rem(group + groups - k, groups)
                        first = pl.multiple_of(lax.rem(origin, spans) * span, 128)
                        row = pl.multiple_of(origin // spans * proj, proj)
                        x[pl.ds(row, proj), pl.ds(first, span)] = given[k][...]
                for i, grad in enumerate((top, bottom)):
                    y = nt(grad[...], x[...])
                    for k in range(parts):
                        left = side_of(target_of(part, k)) == 0
                        outs[k][:, i * proj : (i + 1) * proj] = jnp.where(left, y[:, :proj], y[:, proj:]).astype(BF16)

        return launch(
            body,
            [(info, SMEM)] + [(v, VMEM) for v in below_grad] + [(s, VMEM) for s in sources],
            [((half, 2 * proj), BF16, VMEM)] * parts,
            [pltpu.VMEM((2 * proj, local), BF16)],
            after,
            8,
        )

    def inputs_side(info, saved, signs, down, low_bits, *rest):
        outs, (saved_buf, both, sems) = rest[:parts], rest[parts:]
        part = info[2]
        finish(copies(sems, (saved, saved_buf)))
        both[:proj, :] = nt(signs[...], saved_buf[...])
        reduced = nn(saved_buf[...], down[...])
        both[proj:, :] = nt(signs_of(low_bits[...]).T[proj:, :], reduced, BEST)
        for k in range(parts):
            first = pl.multiple_of(target_of(part, k) * share, share)
            outs[k][...] = both[pl.ds(first, share), :]

    scale = ADAPTER_SCALE / math.sqrt(seq) / math.sqrt(width) / math.sqrt(rank)

    def features(info, lengths, own_top, own_bottom, *rest):
        xs, ys, (out, y) = rest[:parts], rest[parts : (last + 1) * parts], rest[(last + 1) * parts :]
        total = ys[0][...].astype(F32)
        for value in ys[1:]:
            total += value[...].astype(F32)
        y[:half, :] = total[:, :proj]
        y[half:, :] = total[:, proj:]

        @pl.when(info[0] == last)
        def _():
            left = side_of(info[2]) == 0
            y[:half, :] = jnp.where(left, own_top[:, :proj], own_top[:, proj:])
            y[half:, :] = jnp.where(left, own_bottom[:, :proj], own_bottom[:, proj:])

        x = xs[0][...]
        for value in xs[1:]:
            x += value[...]
        starts = packed_at(lengths, count)
        for e in range(count):
            real = lengths[e]
            left = x[:, e * seq : (e + 1) * seq] * scale
            left = jnp.where(lax.broadcasted_iota(jnp.int32, left.shape, 1) < real, left, 0.0)
            right = y[pl.ds(pl.multiple_of(starts[e], ROWS), seq), :]
            right = jnp.where(lax.broadcasted_iota(jnp.int32, right.shape, 0) < real, right, 0.0)
            out[e] = nn(left, right, BEST)

    signs, up_low, *packed = launch(
        prepare,
        [(info, SMEM), (lengths, SMEM), (bits, HBM), (rank_sign_bits, VMEM), (up, HBM), (output_gradient, HBM)],
        [((proj, local), BF16, VMEM)] * 2 + [((half, local), BF16, VMEM)] * 2,
        [
            pltpu.VMEM((proj, local), jnp.int32),
            pltpu.VMEM((rank, local), BF16),
            pltpu.VMEM((count, seq, local), BF16),
            pltpu.SemaphoreType.DMA((2 + count,)),
        ],
    )
    below = [None] * stages
    for s in range(last - 2, -1, -1):
        below[s + 1] = shift(up_low, [(s, s + 1)], same, 0)
    others = [[shift(packed[i], [(last, last)], same, -k) for k in range(1, parts)] for i in (1, 0)][::-1]
    total, u_part, y_part = launch(
        push_own,
        [(info, SMEM), (lengths, SMEM)] + [(v, VMEM) for v in packed] + [(weight, HBM), (up, HBM), (signs, VMEM)],
        [((tokens, local), F32, VMEM), ((tokens, rank), F32, VMEM), ((tokens, proj), F32, VMEM)],
        [
            pltpu.VMEM((rank + proj, local), BF16),
            pltpu.VMEM((ring, block, local), BF16),
            pltpu.SemaphoreType.DMA((1,)),
            pltpu.SemaphoreType.DMA((ring,)),
        ],
    )

    def rest_of(which, after):
        return launch(
            push_rest(which),
            [(info, SMEM), (lengths, SMEM), (bits, HBM), (rank_sign_bits, VMEM)]
            + [(weight, HBM), (up, HBM), (down, VMEM), (total, VMEM), (u_part, VMEM), (y_part, VMEM)]
            + [(value, VMEM) for value in others[which]],
            [((half, local), BF16, VMEM), ((half, 2 * proj), F32, VMEM)],
            [
                pltpu.VMEM((parts - 1, proj, local), jnp.int32),
                pltpu.VMEM((parts - 1, rank + proj, local), BF16),
                pltpu.VMEM((half, rank), BF16),
                pltpu.VMEM((half, block), F32),
                pltpu.VMEM((ring, block, local), BF16),
                pltpu.SemaphoreType.DMA((2 * (parts - 1),)),
                pltpu.SemaphoreType.DMA((ring,)),
            ],
            after,
        )

    below_top, own_top = rest_of(0, [])
    *outs, held = launch(
        first_step,
        [(info, SMEM), (weight, HBM), (down, VMEM), (up, HBM), (below[1], VMEM), (signs, VMEM)],
        [((proj, span), BF16, VMEM)] * parts + [((far_count, local, piece), BF16, VMEM)],
        [
            pltpu.VMEM((proj, local), BF16),
            pltpu.VMEM((proj, rank), BF16),
            pltpu.VMEM((parts, rank, span), BF16),
            pltpu.SemaphoreType.DMA((far_count,)),
            pltpu.SemaphoreType.DMA((parts,)),
        ],
        [own_top],
        6,
    )
    arrived = [shift(v, [(1, 2)], neighbour(z), k) for z in range(spans) for k, v in enumerate(outs)]
    *far_outs, x, low = launch(
        second_far,
        [(info, SMEM), (held, VMEM), (down, VMEM), (up, HBM)]
        + [(v, VMEM) for v in arrived + [below[2], signs]],
        [((proj, span), BF16, VMEM), ((2 * proj, span), BF16, VMEM)] * len(far_targets)
        + [((wide, local), BF16, VMEM), ((wide, rank), BF16, VMEM)],
        [
            pltpu.VMEM((len(far_targets), rank, span), BF16),
            pltpu.SemaphoreType.DMA((len(far_targets),)),
        ],
        room=12,
    )
    near_outs = launch(
        second_near,
        [(info, SMEM), (weight, HBM), (up, HBM), (x, VMEM), (low, VMEM)],
        [((proj, span), BF16, VMEM), ((2 * proj, span), BF16, VMEM)] * len(near_targets),
        [
            pltpu.VMEM((near_count, local, piece), BF16),
            pltpu.VMEM((len(near_targets), rank, span), BF16),
            pltpu.SemaphoreType.DMA((near_count,)),
            pltpu.SemaphoreType.DMA((len(near_targets),)),
        ],
        [far_outs[0]],
        20,
    )
    outs = list(near_outs) + list(far_outs)
    second = [shift(v, [(2, 2)], same, k) if k else v for k, v in enumerate(outs[::2])]
    direct, _ = lax.optimization_barrier((outs[1::2], near_outs[0]))
    direct = [shift(v, [(2, 2)], same, k) if k else v for k, v in enumerate(direct)]
    reach_zero = added(second)
    direct, _ = lax.optimization_barrier((direct, reach_zero))
    reach_one = added(direct)
    reach_one = [shift(reach_one, [(2, last)], neighbour(z), 0) for z in range(spans)]
    reach_zero = [shift(reach_zero, [(2, last)], further(k), 0) for k in range(groups)]
    below_bottom, own_bottom = rest_of(1, [near_outs[0]])
    below_grad = [below_top, below_bottom]
    up_low, _ = lax.optimization_barrier((up_low, near_outs[0]))
    below[last] = shift(up_low, [(last - 1, last)], same, 0)

    y_all = []
    to_two = meet("here", [below[last], signs])
    y_all += [shift(v, [(last, 2)], same, k) for k, v in enumerate(to_two)]
    to_one = meet("spans", reach_one, [to_two[0]])
    y_all += [shift(v, [(last, 1)], same, k) for k, v in enumerate(to_one)]
    to_zero = meet("all", reach_zero, [to_one[0]])
    y_all += [shift(v, [(last, 0)], same, k) for k, v in enumerate(to_zero)]
    x_all = launch(
        inputs_side,
        [
            (info, SMEM),
            (acts[:, 0].reshape(tokens, local), HBM),
            (signs, VMEM),
            (down, VMEM),
            (rank_sign_bits, VMEM),
        ],
        [((share, tokens), F32, VMEM)] * parts,
        [
            pltpu.VMEM((tokens, local), BF16),
            pltpu.VMEM((2 * proj, tokens), F32),
            pltpu.SemaphoreType.DMA((1,)),
        ],
        [to_zero[0]],
    )
    x_all = [
        lax.ppermute(v, "tensor", [(q, (q + k) % parts) for q in range(parts)]) if k else v
        for k, v in enumerate(x_all)
    ]
    (feats,) = launch(
        features,
        [(info, SMEM), (lengths, SMEM), (own_top, VMEM), (own_bottom, VMEM)] + [(x, VMEM) for x in x_all] + [(y, VMEM) for y in y_all],
        [((count, share, proj), F32, VMEM)],
        [pltpu.VMEM((tokens, proj), F32)],
    )
    return feats.reshape(count, 1, share * proj)


def solution(mesh):
    placed = (
        P("dp", None, "tensor"),
        P("dp", "pipe", None, "tensor"),
        P("pipe", "tensor", None),
        P("pipe", "tensor", None),
        P("pipe", None, None),
        P(),
        P(),
        P("dp"),
    )
    return jax.shard_map(
        per_device, mesh=mesh, in_specs=placed, out_specs=P("dp", "pipe", "tensor"), check_vma=False
    )
```

```python
import math

import jax
import jax.numpy as jnp
from jax import lax
from jax.experimental import pallas as pl
from jax.experimental.pallas import tpu as pltpu
from jax.sharding import PartitionSpec as P

ADAPTER_SCALE = 2.0
AXES = ("pipe", "dp", "tensor")
F32 = jnp.float32
BF16 = jnp.bfloat16
SMEM, VMEM, HBM, ANY = pltpu.SMEM, pltpu.VMEM, pltpu.HBM, pl.ANY
ROWS = 16
BEST = lax.Precision.HIGHEST


def nt(left, right, precision=None):
    return lax.dot_general(
        left, right, (((1,), (1,)), ((), ())), precision=precision, preferred_element_type=F32
    )


def nn(left, right, precision=None):
    return jnp.dot(left, right, precision=precision, preferred_element_type=F32)


def placed(array, space):
    return pltpu.with_memory_space_constraint(array, HBM) if space is HBM else array


def launch(body, ins, outs, scratch=(), after=(), room=8):
    count, extra = len(ins), len(after)

    def kernel(*refs):
        body(*refs[:count], *refs[count + extra :])

    return pl.pallas_call(
        kernel,
        in_specs=[pl.BlockSpec(memory_space=space) for _, space in ins]
        + [pl.BlockSpec(memory_space=ANY)] * extra,
        out_specs=[pl.BlockSpec(memory_space=space) for _, _, space in outs],
        out_shape=[
            pltpu.HBM(shape, dtype) if space is HBM else jax.ShapeDtypeStruct(shape, dtype)
            for shape, dtype, space in outs
        ],
        scratch_shapes=list(scratch),
        compiler_params=pltpu.CompilerParams(vmem_limit_bytes=room * 2**20),
        cost_estimate=pl.CostEstimate(flops=0, bytes_accessed=0, transcendentals=0),
    )(*[placed(array, space) for array, space in ins], *after)


def shift(value, routes, to_group, by_tensor):
    groups, parts = lax.axis_size("dp"), lax.axis_size("tensor")

    def place(stage, group, part):
        return (stage * groups + group) * parts + part % parts

    pairs = [
        (place(source, g, k), place(target, to_group(g), k + by_tensor))
        for source, target in routes
        for g in range(groups)
        for k in range(parts)
    ]
    return lax.ppermute(value, AXES, pairs)


def copies(sems, *pairs):
    made = [pltpu.make_async_copy(source, target, sems.at[i]) for i, (source, target) in enumerate(pairs)]
    for copy in made:
        copy.start()
    return made


def finish(made):
    for copy in made:
        copy.wait()


def packed_at(lengths, count):
    starts = [jnp.int32(0)]
    for e in range(count):
        starts.append(starts[-1] + (lengths[e] + ROWS - 1) // ROWS * ROWS)
    return starts


def by_rows(rows, sizes, step):
    least = 0
    for size in sizes:
        pl.when((rows > least) & (rows <= size))(lambda size=size: step(size))
        least = size


def per_device(
    output_gradient,
    acts,
    weights,
    adapter_down_factors,
    adapter_up_factors,
    feature_sign_bits,
    rank_sign_bits,
    lengths,
):
    stages, groups, parts = (lax.axis_size(name) for name in AXES)
    last = stages - 1
    count, seq, local = output_gradient.shape
    tokens = count * seq
    half = tokens // 2
    width = local * parts
    rank = adapter_up_factors.shape[1]
    proj = feature_sign_bits.shape[1]
    share = 2 * proj // parts
    block = min(256, local)
    assert local % block == 0 and seq % ROWS == 0
    spans = groups // 2
    span = local // spans
    piece = min(512, span)
    per_span = span // piece
    weight, down, up = weights[0], adapter_down_factors[0], adapter_up_factors[0]
    bits = feature_sign_bits.T
    info = jnp.stack([lax.axis_index(name) for name in AXES]).astype(jnp.int32)

    def target_of(part, k):
        return lax.rem(part + k, parts)

    def origin_of(group, k):
        return lax.rem(lax.rem(group, spans) + spans - k, spans)

    def neighbour(k):
        return lambda g: g // spans * spans + (g + k) % spans

    def further(k):
        return lambda g: (g + k) % groups

    def same(g):
        return g

    def columns(which):
        return pl.ds(pl.multiple_of(which * local, 128), local)

    def side_of(part):
        return part // (parts // 2)

    def signs_of(values):
        return (2 * values - 1).astype(F32)

    def prepare(info, bits, low_bits, up, signs, up_low, low_buf, bits_buf, up_buf, sems):
        mine = columns(info[2])
        made = copies(sems, (low_bits, low_buf), (up.at[:, mine], up_buf), (bits.at[:, mine], bits_buf))
        made[0].wait()
        low_left = signs_of(low_buf[...]).T[:proj, :].astype(BF16)
        made[1].wait()
        up_low[...] = nn(low_left, up_buf[...]).astype(BF16)
        made[2].wait()
        signs[...] = signs_of(bits_buf[...]).astype(BF16)

    def pack(lengths, source, target):
        starts = packed_at(lengths, count)
        for e in range(count):
            target[pl.ds(pl.multiple_of(starts[e], ROWS), seq), :] = source[e * seq : (e + 1) * seq, :]

    near_targets, far_targets = list(range(max(1, parts // 2))), list(range(max(1, parts // 2), parts))
    slots = 3
    far_count, near_count = len(far_targets) * per_span, len(near_targets) * per_span

    order = far_targets + near_targets

    def fetches(info, weight, buffer, sems, first, end):
        made = []
        for i in range(first, end):
            column = (
                target_of(info[2], order[i // per_span]) * local
                + lax.rem(info[1], spans) * span
                + i % per_span * piece
            )
            where = pl.ds(pl.multiple_of(column, 128), piece)
            slot = (i - first) % buffer.shape[0]
            made.append(pltpu.make_async_copy(weight.at[:, where], buffer.at[slot], sems.at[slot]))
        return made

    def lookups(info, up, up_buf, sems, targets):
        pairs = []
        for i, k in enumerate(targets):
            column = target_of(info[2], k) * local + lax.rem(info[1], spans) * span
            pairs.append((up.at[:, pl.ds(pl.multiple_of(column, 128), span)], up_buf.at[i]))
        return copies(sems, *pairs)

    def in_turn(made, ahead, use):
        for copy in made[:ahead]:
            copy.start()
        for i, copy in enumerate(made):
            copy.wait()
            if i + ahead < len(made):
                made[i + ahead].start()
            use(i)

    def first_step(info, weight, down, up, even, signs, *rest):
        outs, (held, x, low, down_buf, up_buf, sems, up_sems) = rest[:parts], rest[parts:]
        stage, group = info[0], info[1]

        @pl.when(stage == 1)
        def _():
            made = fetches(info, weight, held, sems, 0, far_count + near_count)
            ready = lookups(info, up, up_buf, up_sems, order)
            down_copy = pltpu.make_async_copy(down, down_buf, up_sems.at[parts])
            down_copy.start()
            x[...] = jnp.where(group < spans, even[...], signs[...])

            def use(i):
                if i == 0:
                    down_copy.wait()
                    low[...] = (ADAPTER_SCALE * nn(x[...], down_buf[...])).astype(BF16)
                    finish(ready)
                at = pl.ds(i % per_span * piece, piece)
                total = nn(x[...], held[i % far_count]) + nn(low[...], up_buf[i // per_span, :, at])
                outs[order[i // per_span]][:, at] = total.astype(BF16)

            in_turn(made, min(slots, far_count - 1), use)

        @pl.when(stage == 2)
        def _():
            in_turn(fetches(info, weight, held, sems, 0, far_count), far_count, lambda i: None)

    wide = 3 * proj

    def second_far(info, held, down, up, *rest):
        given, rest = rest[: spans * parts + 2], rest[spans * parts + 2 :]
        outs, (x, low, down_buf, up_buf, up_sems) = rest[: len(far_targets)], rest[len(far_targets) :]
        group = info[1]

        @pl.when(info[0] == 2)
        def _():
            ready = lookups(info, up, up_buf, up_sems, far_targets)
            down_copy = pltpu.make_async_copy(down, down_buf, up_sems.at[len(far_targets)])
            down_copy.start()
            for k in range(spans):
                total = given[k * parts][...].astype(F32)
                for value in given[k * parts + 1 : (k + 1) * parts]:
                    total += value[...].astype(F32)
                first = pl.multiple_of(origin_of(group, k) * span, 128)
                x[:proj, pl.ds(first, span)] = total.astype(BF16)
            x[proj : 2 * proj, :] = given[-2][...]
            x[2 * proj :, :] = given[-1][...]
            down_copy.wait()
            low[...] = (ADAPTER_SCALE * nn(x[...], down_buf[...])).astype(BF16)
            finish(ready)
            for i in range(len(far_targets) * per_span):
                at = pl.ds(i % per_span * piece, piece)
                total = nn(x[...], held[i]) + nn(low[...], up_buf[i // per_span, :, at])
                outs[i // per_span][:, at] = total.astype(BF16)

    def second_near(info, weight, up, x, low, *rest):
        outs, (w, up_buf, sems, up_sems) = rest[: len(near_targets)], rest[len(near_targets) :]

        @pl.when(info[0] == 2)
        def _():
            made = fetches(info, weight, w, sems, far_count, far_count + near_count)
            ready = lookups(info, up, up_buf, up_sems, near_targets)

            def use(i):
                if i == 0:
                    finish(ready)
                at = pl.ds(i % per_span * piece, piece)
                total = nn(x[...], w[i % slots]) + nn(low[...], up_buf[i // per_span, :, at])
                outs[i // per_span][:, at] = total.astype(BF16)

            in_turn(made, slots - 1, use)

    def added(values):
        total = values[0].astype(F32)
        for value in values[1:]:
            total += value.astype(F32)
        return total.astype(BF16)

    blocks, ring = local // block, 5

    def stream(weight, ring_buf, sems, count_of, part_of, use):
        def fetch(n):
            i, k = n // count_of, n % count_of
            first = pl.multiple_of(i * block, block)
            slot = lax.rem(n, ring)
            return pltpu.make_async_copy(
                weight.at[pl.ds(first, block), columns(part_of(k))], ring_buf.at[slot], sems.at[slot]
            )

        total_steps = blocks * count_of
        for n in range(min(ring - 1, total_steps)):
            fetch(jnp.int32(n)).start()

        def step(n, _):
            fetch(n).wait()

            @pl.when(n + ring - 1 < total_steps)
            def _():
                fetch(n + ring - 1).start()

            use(n // count_of, n % count_of, lax.rem(n, ring))
            return 0

        return lambda: lax.fori_loop(0, total_steps, step, 0)

    sizes = range(half, tokens + 1, tokens // 8)

    sizes = range(half, tokens + 1, tokens // 8)

    def push_own(info, lengths, raw, bits, weight, up, signs, total, u_part, y_part, both_next, *rest):
        grad, bits_buf, both, ring_buf, sems, ring_sems, tile_sems = rest
        part = info[2]

        @pl.when(info[0] == last)
        def _():
            rows = packed_at(lengths, count)[count]

            def use(i, k, slot):
                at = pl.ds(pl.multiple_of(i * block, block), block)

                def sized(size):
                    total[:size, at] = nt(grad[:size], ring_buf[slot])

                by_rows(rows, sizes, sized)

            starts = packed_at(lengths, count)
            tiles = []
            for e in range(count):
                for j in range(seq // ROWS):
                    there = pl.ds(pl.multiple_of(starts[e] + ROWS * j, ROWS), ROWS)
                    here = pl.ds(e * seq + ROWS * j, ROWS)
                    copy = pltpu.make_async_copy(raw.at[here], grad.at[there], tile_sems.at[len(tiles)])
                    tiles.append((ROWS * j < lengths[e], copy))
            for real, copy in tiles:
                pl.when(real)(copy.start)
            pairs = [(up.at[:, columns(part)], both.at[:rank])]
            for k in range(parts - 1):
                there = columns(target_of(part, k + 1))
                pairs += [(up.at[:, there], both_next.at[k, :rank]), (bits.at[:, there], bits_buf.at[k])]
            made = copies(sems, *pairs)
            go = stream(weight, ring_buf, ring_sems, 1, lambda k: part, use)
            both[rank:, :] = signs[...]
            finish(made)
            for real, copy in tiles:
                pl.when(real)(copy.wait)
            for k in range(parts - 1):
                both_next[k, rank:, :] = signs_of(bits_buf[k]).astype(BF16)
            low = nt(grad[...], both[...])
            u_part[...], y_part[...] = low[:, :rank], low[:, rank:]
            go()

    def push_rest(info, lengths, low_bits, weight, down, total, u_part, y_part, both_next, *rest):
        given, rest = rest[: parts - 1], rest[parts - 1 :]
        below, own, grad, u_all, so_far, ring_buf, ring_sems = rest
        part = info[2]

        @pl.when(info[0] == last)
        def _():
            rows = packed_at(lengths, count)[count]

            def use(i, k, slot):
                at = pl.ds(pl.multiple_of(i * block, block), block)

                def sized(size):
                    for j in range(parts - 1):

                        @pl.when(k == j)
                        def _(j=j):
                            value = nt(grad[j, :size], ring_buf[slot])
                            if j == 0:
                                value += total[:size, at]
                                value += ADAPTER_SCALE * nt(u_all[:size], down[at, :])
                            else:
                                value += so_far[:size]
                            if j == parts - 2:
                                below[:size, at] = value.astype(BF16)
                            else:
                                so_far[:size] = value

                by_rows(rows, sizes, sized)

            go = stream(weight, ring_buf, ring_sems, parts - 1, lambda k: lax.rem(part + k + 1, parts), use)
            u_sum, y_sum = u_part[...], y_part[...]
            for k in range(parts - 1):
                pack(lengths, given[k], grad.at[k])
                low = nt(grad[k], both_next[k])
                u_sum += low[:, :rank]
                y_sum += low[:, rank:]
            u_all[...] = u_sum.astype(BF16)
            low_left = signs_of(low_bits[...]).T[:proj, :].astype(BF16)
            own[:, :proj] = nt(u_all[...], low_left)
            own[:, proj:] = y_sum
            go()

    def inputs_side(info, saved, signs, down, low_bits, *rest):
        outs, (saved_buf, down_buf, low_buf, both, sems) = rest[:parts], rest[parts:]
        finish(copies(sems, (saved, saved_buf), (down, down_buf), (low_bits, low_buf)))
        both[:proj, :] = nt(signs[...], saved_buf[...])
        reduced = nn(saved_buf[...], down_buf[...])
        both[proj:, :] = nt(signs_of(low_buf[...]).T[proj:, :], reduced, BEST)
        for k in range(parts):
            first = pl.multiple_of(target_of(info[2], k) * share, share)
            outs[k][...] = both[pl.ds(first, share), :]

    scale = ADAPTER_SCALE / math.sqrt(seq) / math.sqrt(width) / math.sqrt(rank)

    def features(info, lengths, own, *rest):
        xs, ys, (out, y) = rest[:parts], rest[parts : (last + 1) * parts], rest[(last + 1) * parts :]
        total = ys[0][...].astype(F32)
        for value in ys[1:]:
            total += value[...].astype(F32)
        y[:half, :] = total[:, :proj]
        y[half:, :] = total[:, proj:]

        @pl.when(info[0] == last)
        def _():
            left = side_of(info[2]) == 0
            y[...] = jnp.where(left, own[:, :proj], own[:, proj:])

        x = xs[0][...]
        for value in xs[1:]:
            x += value[...]
        starts = packed_at(lengths, count)
        for e in range(count):
            real = lengths[e]
            left = x[:, e * seq : (e + 1) * seq] * scale
            left = jnp.where(lax.broadcasted_iota(jnp.int32, left.shape, 1) < real, left, 0.0)
            right = y[pl.ds(pl.multiple_of(starts[e], ROWS), seq), :]
            right = jnp.where(lax.broadcasted_iota(jnp.int32, right.shape, 0) < real, right, 0.0)
            out[e] = nn(left, right, BEST)

    signs, up_low = launch(
        prepare,
        [(info, SMEM), (bits, HBM), (rank_sign_bits, HBM), (up, HBM)],
        [((proj, local), BF16, VMEM)] * 2,
        [
            pltpu.VMEM(rank_sign_bits.shape, jnp.int32),
            pltpu.VMEM((proj, local), jnp.int32),
            pltpu.VMEM((rank, local), BF16),
            pltpu.SemaphoreType.DMA((3,)),
        ],
        room=8,
    )
    grad = output_gradient.reshape(tokens, local)
    grad_late, _ = lax.optimization_barrier((grad, up_low))
    others = [shift(grad_late, [(last, last)], same, -k) for k in range(1, parts)]
    below = [None] + [shift(up_low, [(s, s + 1)], same, 0) for s in range(last - 1, -1, -1)][::-1]
    total, u_part, y_part, both_next = launch(
        push_own,
        [(info, SMEM), (lengths, SMEM), (grad, HBM), (bits, HBM), (weight, HBM), (up, HBM), (signs, VMEM)],
        [((tokens, local), F32, VMEM), ((tokens, rank), F32, VMEM), ((tokens, proj), F32, VMEM)]
        + [((parts - 1, rank + proj, local), BF16, VMEM)],
        [
            pltpu.VMEM((tokens, local), BF16),
            pltpu.VMEM((parts - 1, proj, local), jnp.int32),
            pltpu.VMEM((rank + proj, local), BF16),
            pltpu.VMEM((ring, block, local), BF16),
            pltpu.SemaphoreType.DMA((2 * parts,)),
            pltpu.SemaphoreType.DMA((ring,)),
            pltpu.SemaphoreType.DMA((tokens // ROWS,)),
        ],
        room=20,
    )
    *outs, held = launch(
        first_step,
        [(info, SMEM), (weight, HBM), (down, HBM), (up, HBM), (below[1], VMEM), (signs, VMEM)],
        [((proj, span), BF16, VMEM)] * parts + [((far_count, local, piece), BF16, VMEM)],
        [
            pltpu.VMEM((proj, local), BF16),
            pltpu.VMEM((proj, rank), BF16),
            pltpu.VMEM((local, rank), BF16),
            pltpu.VMEM((parts, rank, span), BF16),
            pltpu.SemaphoreType.DMA((far_count,)),
            pltpu.SemaphoreType.DMA((parts + 1,)),
        ],
        [u_part],
        9,
    )
    arrived = [shift(v, [(1, 2)], neighbour(z), k) for z in range(spans) for k, v in enumerate(outs)]
    x_all = launch(
        inputs_side,
        [
            (info, SMEM),
            (acts[:, 0].reshape(tokens, local), HBM),
            (signs, VMEM),
            (down, HBM),
            (rank_sign_bits, HBM),
        ],
        [((share, tokens), F32, VMEM)] * parts,
        [
            pltpu.VMEM((tokens, local), BF16),
            pltpu.VMEM((local, rank), BF16),
            pltpu.VMEM(rank_sign_bits.shape, jnp.int32),
            pltpu.VMEM((2 * proj, tokens), F32),
            pltpu.SemaphoreType.DMA((3,)),
        ],
        [outs[0]],
        10,
    )
    x_all = [
        lax.ppermute(v, "tensor", [(q, (q + k) % parts) for q in range(parts)]) if k else v
        for k, v in enumerate(x_all)
    ]
    *far_outs, x, low = launch(
        second_far,
        [(info, SMEM), (held, VMEM), (down, HBM), (up, HBM)]
        + [(v, VMEM) for v in arrived + [below[2], signs]],
        [((wide, span), BF16, VMEM)] * len(far_targets)
        + [((wide, local), BF16, VMEM), ((wide, rank), BF16, VMEM)],
        [
            pltpu.VMEM((local, rank), BF16),
            pltpu.VMEM((len(far_targets), rank, span), BF16),
            pltpu.SemaphoreType.DMA((len(far_targets) + 1,)),
        ],
        [x_all[0]],
        12,
    )
    near_outs = launch(
        second_near,
        [(info, SMEM), (weight, HBM), (up, HBM), (x, VMEM), (low, VMEM)],
        [((wide, span), BF16, VMEM)] * len(near_targets),
        [
            pltpu.VMEM((slots, local, piece), BF16),
            pltpu.VMEM((len(near_targets), rank, span), BF16),
            pltpu.SemaphoreType.DMA((slots,)),
            pltpu.SemaphoreType.DMA((len(near_targets),)),
        ],
        [far_outs[0]],
        17,
    )
    outs = list(near_outs) + list(far_outs)
    both_reach = added([shift(v, [(2, 2)], same, k) if k else v for k, v in enumerate(outs)])
    reach_zero, reach_one = both_reach[:proj], both_reach[proj:]
    reach_one_kept, reach_zero_kept = reach_one, reach_zero
    reach_one = [shift(reach_one, [(2, last)], neighbour(z), 0) for z in range(1, spans)]
    reach_zero = [shift(reach_zero, [(2, last)], further(k), 0) for k in range(1, groups)]
    below_grad, own = launch(
        push_rest,
        [(info, SMEM), (lengths, SMEM), (rank_sign_bits, VMEM), (weight, HBM), (down, VMEM)]
        + [(v, VMEM) for v in [total, u_part, y_part, both_next] + others],
        [((tokens, local), BF16, VMEM), ((tokens, 2 * proj), F32, VMEM)],
        [
            pltpu.VMEM((parts - 1, tokens, local), BF16),
            pltpu.VMEM((tokens, rank), BF16),
            pltpu.VMEM((tokens, block), F32),
            pltpu.VMEM((ring, block, local), BF16),
            pltpu.SemaphoreType.DMA((ring,)),
        ],
        [reach_one_kept, below[last]],
        18,
    )
    reach_one_kept, reach_zero_kept, reach_one, reach_zero, _ = lax.optimization_barrier(
        (reach_one_kept, reach_zero_kept, reach_one, reach_zero, own)
    )
    reach_zero = [shift(reach_zero_kept, [(2, last)], same, 0)] + reach_zero
    reach_one = [shift(reach_one_kept, [(2, last)], same, 0)] + reach_one

    def meet(info, grad, low_last, signs, *rest):
        ones, zeros = rest[:spans], rest[spans : spans + groups]
        outs, (x,) = rest[spans + groups : -1], rest[-1:]
        group, part = info[1], info[2]

        @pl.when(info[0] == last)
        def _():
            for k in range(groups):
                origin = lax.rem(group + groups - k, groups)
                first = pl.multiple_of(lax.rem(origin, spans) * span, 128)
                row = pl.multiple_of(origin // spans * proj, proj)
                x[pl.ds(row, proj), pl.ds(first, span)] = zeros[k][...]
            for k in range(spans):
                first = pl.multiple_of(origin_of(group, k) * span, 128)
                x[2 * proj : 4 * proj, pl.ds(first, span)] = ones[k][...]
            x[4 * proj : 5 * proj, :] = low_last[...]
            x[5 * proj :, :] = signs[...]
            y = nt(grad[...], x[...])
            for s in range(last):
                left, right = (y[:, (2 * s + i) * proj : (2 * s + i + 1) * proj] for i in range(2))
                for k in range(parts):
                    chosen = jnp.where(side_of(target_of(part, k)) == 0, left, right).astype(BF16)
                    outs[s * parts + k][:, :proj] = chosen[:half]
                    outs[s * parts + k][:, proj:] = chosen[half:]

    y_all = launch(
        meet,
        [(info, SMEM)] + [(v, VMEM) for v in [below_grad, below[last], signs] + reach_one + reach_zero],
        [((half, 2 * proj), BF16, VMEM)] * (last * parts),
        [pltpu.VMEM((2 * last * proj, local), BF16)],
        room=10,
    )
    y_all = [shift(v, [(last, i // parts)], same, i % parts) for i, v in enumerate(y_all)]
    (feats,) = launch(
        features,
        [(info, SMEM), (lengths, SMEM), (own, VMEM)] + [(x, VMEM) for x in x_all] + [(y, VMEM) for y in y_all],
        [((count, share, proj), F32, VMEM)],
        [pltpu.VMEM((tokens, proj), F32)],
        room=8,
    )
    return feats.reshape(count, 1, share * proj)


def solution(mesh):
    placed = (
        P("dp", None, "tensor"),
        P("dp", "pipe", None, "tensor"),
        P("pipe", "tensor", None),
        P("pipe", "tensor", None),
        P("pipe", None, None),
        P(),
        P(),
        P("dp"),
    )
    return jax.shard_map(
        per_device, mesh=mesh, in_specs=placed, out_specs=P("dp", "pipe", "tensor"), check_vma=False
    )
```

```python
import math

import jax
import jax.numpy as jnp
from jax import lax
from jax.experimental import pallas as pl
from jax.experimental.pallas import tpu as pltpu
from jax.sharding import PartitionSpec as P

ADAPTER_SCALE = 2.0
AXES = ("pipe", "dp", "tensor")
F32 = jnp.float32
BF16 = jnp.bfloat16
SMEM, VMEM, HBM, ANY = pltpu.SMEM, pltpu.VMEM, pltpu.HBM, pl.ANY
ROWS = 16
BEST = lax.Precision.HIGHEST


def nt(left, right, precision=None):
    return lax.dot_general(
        left, right, (((1,), (1,)), ((), ())), precision=precision, preferred_element_type=F32
    )


def nn(left, right, precision=None):
    return jnp.dot(left, right, precision=precision, preferred_element_type=F32)


def placed(array, space):
    return pltpu.with_memory_space_constraint(array, HBM) if space is HBM else array


def launch(body, ins, outs, scratch=(), after=(), room=8):
    count, extra = len(ins), len(after)

    def kernel(*refs):
        body(*refs[:count], *refs[count + extra :])

    return pl.pallas_call(
        kernel,
        in_specs=[pl.BlockSpec(memory_space=space) for _, space in ins]
        + [pl.BlockSpec(memory_space=ANY)] * extra,
        out_specs=[pl.BlockSpec(memory_space=space) for _, _, space in outs],
        out_shape=[
            pltpu.HBM(shape, dtype) if space is HBM else jax.ShapeDtypeStruct(shape, dtype)
            for shape, dtype, space in outs
        ],
        scratch_shapes=list(scratch),
        compiler_params=pltpu.CompilerParams(vmem_limit_bytes=room * 2**20),
        cost_estimate=pl.CostEstimate(flops=0, bytes_accessed=0, transcendentals=0),
    )(*[placed(array, space) for array, space in ins], *after)


def shift(value, routes, to_group, by_tensor):
    groups, parts = lax.axis_size("dp"), lax.axis_size("tensor")

    def place(stage, group, part):
        return (stage * groups + group) * parts + part % parts

    pairs = [
        (place(source, g, k), place(target, to_group(g), k + by_tensor))
        for source, target in routes
        for g in range(groups)
        for k in range(parts)
    ]
    return lax.ppermute(value, AXES, pairs)


def copies(sems, *pairs):
    made = [pltpu.make_async_copy(source, target, sems.at[i]) for i, (source, target) in enumerate(pairs)]
    for copy in made:
        copy.start()
    return made


def finish(made):
    for copy in made:
        copy.wait()


def packed_at(lengths, count):
    starts = [jnp.int32(0)]
    for e in range(count):
        starts.append(starts[-1] + (lengths[e] + ROWS - 1) // ROWS * ROWS)
    return starts


def by_rows(rows, sizes, step):
    least = 0
    for size in sizes:
        pl.when((rows > least) & (rows <= size))(lambda size=size: step(size))
        least = size


def per_device(
    output_gradient,
    acts,
    weights,
    adapter_down_factors,
    adapter_up_factors,
    feature_sign_bits,
    rank_sign_bits,
    lengths,
):
    stages, groups, parts = (lax.axis_size(name) for name in AXES)
    last = stages - 1
    count, seq, local = output_gradient.shape
    tokens = count * seq
    half = tokens // 2
    near_rows = tokens - seq // 2
    width = local * parts
    rank = adapter_up_factors.shape[1]
    proj = feature_sign_bits.shape[1]
    share = 2 * proj // parts
    block = min(256, local)
    assert stages == 4 and groups == 4 and parts % 2 == 0 and local % block == 0 and seq % ROWS == 0
    spans = groups // 2
    span = local // spans
    piece = min(512, span)
    per_span = span // piece
    weight, down, up = weights[0], adapter_down_factors[0], adapter_up_factors[0]
    bits = feature_sign_bits.T
    info = jnp.stack([lax.axis_index(name) for name in AXES]).astype(jnp.int32)

    def target_of(part, k):
        return lax.rem(part + k, parts)

    def origin_of(group, k):
        return lax.rem(lax.rem(group, spans) + spans - k, spans)

    def neighbour(k):
        return lambda g: g // spans * spans + (g + k) % spans

    def across(k):
        return lambda g: g ^ k

    def same(g):
        return g

    def columns(which):
        return pl.ds(pl.multiple_of(which * local, 128), local)

    def side_of(part):
        return part // (parts // 2)

    def signs_of(values):
        return (2 * values - 1).astype(F32)

    def prepare(info, bits, low_bits, up, grad, signs, up_low, near, far, low_buf, bits_buf, up_buf, sems):
        mine = columns(info[2])
        made = copies(sems, (low_bits, low_buf), (up.at[:, mine], up_buf), (bits.at[:, mine], bits_buf))
        near_copy = pltpu.make_async_copy(grad.at[:near_rows], near, sems.at[3])
        far_copy = pltpu.make_async_copy(grad.at[near_rows:], far, sems.at[4])
        pl.when(info[0] == last)(near_copy.start)
        pl.when(info[0] == 0)(far_copy.start)
        made[0].wait()
        low_left = signs_of(low_buf[...]).T[:proj, :].astype(BF16)
        made[1].wait()
        up_low[...] = nn(low_left, up_buf[...]).astype(BF16)
        made[2].wait()
        signs[...] = signs_of(bits_buf[...]).astype(BF16)
        pl.when(info[0] == last)(near_copy.wait)
        pl.when(info[0] == 0)(far_copy.wait)

    def pack(lengths, near, far, target):
        starts = packed_at(lengths, count)
        for e in range(count):
            first, end = e * seq, (e + 1) * seq
            for source, begin, low, high in ((near, 0, first, min(end, near_rows)), (far, near_rows, max(first, near_rows), end)):
                if low < high:
                    there = pl.ds(pl.multiple_of(starts[e] + (low - first), ROWS), high - low)
                    target[there, :] = source[low - begin : high - begin, :]

    near_targets, far_targets = list(range(max(1, parts // 2))), list(range(max(1, parts // 2), parts))
    slots = 3
    far_count, near_count = len(far_targets) * per_span, len(near_targets) * per_span

    order = far_targets + near_targets

    def fetches(info, weight, buffer, sems, first, end):
        made = []
        for i in range(first, end):
            column = (
                target_of(info[2], order[i // per_span]) * local
                + lax.rem(info[1], spans) * span
                + i % per_span * piece
            )
            where = pl.ds(pl.multiple_of(column, 128), piece)
            slot = (i - first) % buffer.shape[0]
            made.append(pltpu.make_async_copy(weight.at[:, where], buffer.at[slot], sems.at[slot]))
        return made

    def lookups(info, up, up_buf, sems, targets):
        pairs = []
        for i, k in enumerate(targets):
            column = target_of(info[2], k) * local + lax.rem(info[1], spans) * span
            pairs.append((up.at[:, pl.ds(pl.multiple_of(column, 128), span)], up_buf.at[i]))
        return copies(sems, *pairs)

    def in_turn(made, ahead, use):
        for copy in made[:ahead]:
            copy.start()
        for i, copy in enumerate(made):
            copy.wait()
            if i + ahead < len(made):
                made[i + ahead].start()
            use(i)

    def first_step(info, weight, down, up, even, signs, *rest):
        outs, (held, x, low, down_buf, up_buf, sems, up_sems) = rest[:parts], rest[parts:]
        stage, group = info[0], info[1]

        @pl.when(stage == 1)
        def _():
            made = fetches(info, weight, held, sems, 0, far_count + near_count)
            ready = lookups(info, up, up_buf, up_sems, order)
            down_copy = pltpu.make_async_copy(down, down_buf, up_sems.at[parts])
            down_copy.start()
            x[...] = jnp.where(group < spans, even[...], signs[...])

            def use(i):
                if i == 0:
                    down_copy.wait()
                    low[...] = (ADAPTER_SCALE * nn(x[...], down_buf[...])).astype(BF16)
                    finish(ready)
                at = pl.ds(i % per_span * piece, piece)
                total = nn(x[...], held[i % far_count]) + nn(low[...], up_buf[i // per_span, :, at])
                outs[order[i // per_span]][:, at] = total.astype(BF16)

            in_turn(made, min(slots, far_count - 1), use)

        @pl.when(stage == 2)
        def _():
            in_turn(fetches(info, weight, held, sems, 0, far_count), far_count, lambda i: None)

    wide = 3 * proj

    def second_far(info, held, down, up, *rest):
        given, rest = rest[: spans * parts + 2], rest[spans * parts + 2 :]
        outs, (x, low, down_buf, up_buf, up_sems) = rest[: len(far_targets)], rest[len(far_targets) :]
        group = info[1]

        @pl.when(info[0] == 2)
        def _():
            ready = lookups(info, up, up_buf, up_sems, far_targets)
            down_copy = pltpu.make_async_copy(down, down_buf, up_sems.at[len(far_targets)])
            down_copy.start()
            for k in range(spans):
                total = given[k * parts][...].astype(F32)
                for value in given[k * parts + 1 : (k + 1) * parts]:
                    total += value[...].astype(F32)
                first = pl.multiple_of(origin_of(group, k) * span, 128)
                x[:proj, pl.ds(first, span)] = total.astype(BF16)
            x[proj : 2 * proj, :] = given[-2][...]
            x[2 * proj :, :] = given[-1][...]
            down_copy.wait()
            low[...] = (ADAPTER_SCALE * nn(x[...], down_buf[...])).astype(BF16)
            finish(ready)
            for i in range(len(far_targets) * per_span):
                at = pl.ds(i % per_span * piece, piece)
                total = nn(x[...], held[i]) + nn(low[...], up_buf[i // per_span, :, at])
                outs[i // per_span][:, at] = total.astype(BF16)

    def second_near(info, weight, up, x, low, *rest):
        outs, (w, up_buf, sems, up_sems) = rest[: len(near_targets)], rest[len(near_targets) :]

        @pl.when(info[0] == 2)
        def _():
            made = fetches(info, weight, w, sems, far_count, far_count + near_count)
            ready = lookups(info, up, up_buf, up_sems, near_targets)

            def use(i):
                if i == 0:
                    finish(ready)
                at = pl.ds(i % per_span * piece, piece)
                total = nn(x[...], w[i % slots]) + nn(low[...], up_buf[i // per_span, :, at])
                outs[i // per_span][:, at] = total.astype(BF16)

            in_turn(made, slots - 1, use)

    def added(values):
        total = values[0].astype(F32)
        for value in values[1:]:
            total += value.astype(F32)
        return total.astype(BF16)

    blocks, ring = local // block, 5

    def stream(weight, ring_buf, sems, count_of, part_of, use):
        def fetch(n):
            i, k = n // count_of, n % count_of
            first = pl.multiple_of(i * block, block)
            slot = lax.rem(n, ring)
            return pltpu.make_async_copy(
                weight.at[pl.ds(first, block), columns(part_of(k))], ring_buf.at[slot], sems.at[slot]
            )

        total_steps = blocks * count_of
        for n in range(min(ring - 1, total_steps)):
            fetch(jnp.int32(n)).start()

        def step(n, _):
            fetch(n).wait()

            @pl.when(n + ring - 1 < total_steps)
            def _():
                fetch(n + ring - 1).start()

            use(n // count_of, n % count_of, lax.rem(n, ring))
            return 0

        return lambda: lax.fori_loop(0, total_steps, step, 0)

    sizes = range(half, tokens + 1, tokens // 16)

    sizes = range(half, tokens + 1, tokens // 16)

    def push_own(info, lengths, raw, bits, weight, up, signs, total, u_part, y_part, both_next, *rest):
        grad, bits_buf, both, ring_buf, sems, ring_sems, tile_sems = rest
        part = info[2]

        @pl.when(info[0] == last)
        def _():
            rows = packed_at(lengths, count)[count]

            def use(i, k, slot):
                at = pl.ds(pl.multiple_of(i * block, block), block)

                def sized(size):
                    total[:size, at] = nt(grad[:size], ring_buf[slot])

                by_rows(rows, sizes, sized)

            starts = packed_at(lengths, count)
            tiles = []
            for e in range(count):
                for j in range(seq // ROWS):
                    there = pl.ds(pl.multiple_of(starts[e] + ROWS * j, ROWS), ROWS)
                    here = pl.ds(e * seq + ROWS * j, ROWS)
                    copy = pltpu.make_async_copy(raw.at[here], grad.at[there], tile_sems.at[len(tiles)])
                    tiles.append((ROWS * j < lengths[e], copy))
            for real, copy in tiles:
                pl.when(real)(copy.start)
            pairs = [(up.at[:, columns(part)], both.at[:rank])]
            for k in range(parts - 1):
                there = columns(target_of(part, k + 1))
                pairs += [(up.at[:, there], both_next.at[k, :rank]), (bits.at[:, there], bits_buf.at[k])]
            made = copies(sems, *pairs)
            go = stream(weight, ring_buf, ring_sems, 1, lambda k: part, use)
            both[rank:, :] = signs[...]
            finish(made)
            for real, copy in tiles:
                pl.when(real)(copy.wait)
            for k in range(parts - 1):
                both_next[k, rank:, :] = signs_of(bits_buf[k]).astype(BF16)
            low = nt(grad[...], both[...])
            u_part[...], y_part[...] = low[:, :rank], low[:, rank:]
            go()

    def push_rest(info, lengths, low_bits, weight, down, total, u_part, y_part, both_next, *rest):
        given, rest = rest[: 2 * (parts - 1)], rest[2 * (parts - 1) :]
        below, own, grad, u_all, so_far, ring_buf, ring_sems = rest
        part = info[2]

        @pl.when(info[0] == last)
        def _():
            rows = packed_at(lengths, count)[count]

            def use(i, k, slot):
                at = pl.ds(pl.multiple_of(i * block, block), block)

                def sized(size):
                    for j in range(parts - 1):

                        @pl.when(k == j)
                        def _(j=j):
                            value = nt(grad[j, :size], ring_buf[slot])
                            if j == 0:
                                value += total[:size, at]
                                value += ADAPTER_SCALE * nt(u_all[:size], down[at, :])
                            else:
                                value += so_far[:size]
                            if j == parts - 2:
                                below[:size, at] = value.astype(BF16)
                            else:
                                so_far[:size] = value

                by_rows(rows, sizes, sized)

            go = stream(weight, ring_buf, ring_sems, parts - 1, lambda k: lax.rem(part + k + 1, parts), use)
            u_sum, y_sum = u_part[...], y_part[...]
            for k in range(parts - 1):
                pack(lengths, given[2 * k], given[2 * k + 1], grad.at[k])
                low = nt(grad[k], both_next[k])
                u_sum += low[:, :rank]
                y_sum += low[:, rank:]
            u_all[...] = u_sum.astype(BF16)
            low_left = signs_of(low_bits[...]).T[:proj, :].astype(BF16)
            own[:, :proj] = nt(u_all[...], low_left)
            own[:, proj:] = y_sum
            go()

    def inputs_side(info, saved, signs, down, low_bits, *rest):
        outs, (saved_buf, down_buf, low_buf, right, both, sems) = rest[:parts], rest[parts:]
        made = copies(sems, (low_bits, low_buf), (down, down_buf), (saved, saved_buf))
        right[:proj, :] = signs[...]
        finish(made[:2])
        turned = nt(signs_of(low_buf[...]).T[proj:, :].astype(BF16), down_buf[...])
        rounded = turned.astype(BF16)
        right[proj : 2 * proj, :] = rounded
        right[2 * proj :, :] = (turned - rounded.astype(F32)).astype(BF16)
        made[2].wait()
        total = nt(right[...], saved_buf[...])
        both[:proj, :] = total[:proj]
        both[proj:, :] = total[proj : 2 * proj] + total[2 * proj :]
        for k in range(parts):
            first = pl.multiple_of(target_of(info[2], k) * share, share)
            outs[k][...] = both[pl.ds(first, share), :]

    scale = ADAPTER_SCALE / math.sqrt(seq) / math.sqrt(width) / math.sqrt(rank)

    def features(info, lengths, own, *rest):
        xs, ys, (out, y) = rest[:parts], rest[parts : (last + 1) * parts], rest[(last + 1) * parts :]
        total = ys[0][...].astype(F32)
        for value in ys[1:]:
            total += value[...].astype(F32)
        y[:half, :] = total[:, :proj]
        y[half:, :] = total[:, proj:]

        @pl.when(info[0] == last)
        def _():
            left = side_of(info[2]) == 0
            y[...] = jnp.where(left, own[:, :proj], own[:, proj:])

        x = xs[0][...]
        for value in xs[1:]:
            x += value[...]
        starts = packed_at(lengths, count)
        for e in range(count):
            real = lengths[e]
            left = x[:, e * seq : (e + 1) * seq] * scale
            left = jnp.where(lax.broadcasted_iota(jnp.int32, left.shape, 1) < real, left, 0.0)
            right = y[pl.ds(pl.multiple_of(starts[e], ROWS), seq), :]
            right = jnp.where(lax.broadcasted_iota(jnp.int32, right.shape, 0) < real, right, 0.0)
            out[e] = nn(left, right, BEST)

    grad = output_gradient.reshape(tokens, local)
    signs, up_low, near, far = launch(
        prepare,
        [(info, SMEM), (bits, HBM), (rank_sign_bits, HBM), (up, HBM), (grad, HBM)],
        [((proj, local), BF16, VMEM)] * 2
        + [((near_rows, local), BF16, VMEM), ((tokens - near_rows, local), BF16, VMEM)],
        [
            pltpu.VMEM(rank_sign_bits.shape, jnp.int32),
            pltpu.VMEM((proj, local), jnp.int32),
            pltpu.VMEM((rank, local), BF16),
            pltpu.SemaphoreType.DMA((5,)),
        ],
        room=8,
    )
    below = [None] + [shift(up_low, [(s, s + 1)], same, 0) for s in range(last - 1, -1, -1)][::-1]
    far, _ = lax.optimization_barrier((far, below[1]))
    fars = [shift(far, [(0, last)], same, -k) for k in range(1, parts)]
    nears = [shift(near, [(last, last)], same, -k) for k in range(1, parts)]
    total, u_part, y_part, both_next = launch(
        push_own,
        [(info, SMEM), (lengths, SMEM), (grad, HBM), (bits, HBM), (weight, HBM), (up, HBM), (signs, VMEM)],
        [((tokens, local), F32, VMEM), ((tokens, rank), F32, VMEM), ((tokens, proj), F32, VMEM)]
        + [((parts - 1, rank + proj, local), BF16, VMEM)],
        [
            pltpu.VMEM((tokens, local), BF16),
            pltpu.VMEM((parts - 1, proj, local), jnp.int32),
            pltpu.VMEM((rank + proj, local), BF16),
            pltpu.VMEM((ring, block, local), BF16),
            pltpu.SemaphoreType.DMA((2 * parts,)),
            pltpu.SemaphoreType.DMA((ring,)),
            pltpu.SemaphoreType.DMA((tokens // ROWS,)),
        ],
        [below[1]],
        room=20,
    )
    *outs, held = launch(
        first_step,
        [(info, SMEM), (weight, HBM), (down, HBM), (up, HBM), (below[1], VMEM), (signs, VMEM)],
        [((proj, span), BF16, VMEM)] * parts + [((far_count, local, piece), BF16, VMEM)],
        [
            pltpu.VMEM((proj, local), BF16),
            pltpu.VMEM((proj, rank), BF16),
            pltpu.VMEM((local, rank), BF16),
            pltpu.VMEM((parts, rank, span), BF16),
            pltpu.SemaphoreType.DMA((far_count,)),
            pltpu.SemaphoreType.DMA((parts + 1,)),
        ],
        [u_part] + fars,
        9,
    )
    arrived = [shift(v, [(1, 2)], neighbour(z), k) for z in range(spans) for k, v in enumerate(outs)]
    x_all = launch(
        inputs_side,
        [
            (info, SMEM),
            (acts[:, 0].reshape(tokens, local), HBM),
            (signs, VMEM),
            (down, HBM),
            (rank_sign_bits, HBM),
        ],
        [((share, tokens), F32, VMEM)] * parts,
        [
            pltpu.VMEM((tokens, local), BF16),
            pltpu.VMEM((local, rank), BF16),
            pltpu.VMEM(rank_sign_bits.shape, jnp.int32),
            pltpu.VMEM((3 * proj, local), BF16),
            pltpu.VMEM((2 * proj, tokens), F32),
            pltpu.SemaphoreType.DMA((3,)),
        ],
        [outs[0]],
        12,
    )
    x_all = [
        lax.ppermute(v, "tensor", [(q, (q + k) % parts) for q in range(parts)]) if k else v
        for k, v in enumerate(x_all)
    ]
    *far_outs, x, low = launch(
        second_far,
        [(info, SMEM), (held, VMEM), (down, HBM), (up, HBM)]
        + [(v, VMEM) for v in arrived + [below[2], signs]],
        [((wide, span), BF16, VMEM)] * len(far_targets)
        + [((wide, local), BF16, VMEM), ((wide, rank), BF16, VMEM)],
        [
            pltpu.VMEM((local, rank), BF16),
            pltpu.VMEM((len(far_targets), rank, span), BF16),
            pltpu.SemaphoreType.DMA((len(far_targets) + 1,)),
        ],
        [x_all[0]],
        12,
    )
    near_outs = launch(
        second_near,
        [(info, SMEM), (weight, HBM), (up, HBM), (x, VMEM), (low, VMEM)],
        [((wide, span), BF16, VMEM)] * len(near_targets),
        [
            pltpu.VMEM((slots, local, piece), BF16),
            pltpu.VMEM((len(near_targets), rank, span), BF16),
            pltpu.SemaphoreType.DMA((slots,)),
            pltpu.SemaphoreType.DMA((len(near_targets),)),
        ],
        [far_outs[0]],
        17,
    )
    outs = list(near_outs) + list(far_outs)
    both_reach = added([shift(v, [(2, 2)], same, k) if k else v for k, v in enumerate(outs)])
    turns = list(range(2, groups)) + [1, 0]
    reach = [shift(both_reach[:proj] if k >= spans else both_reach, [(2, last)], across(k), 0) for k in range(groups)]
    below_grad, own = launch(
        push_rest,
        [(info, SMEM), (lengths, SMEM), (rank_sign_bits, VMEM), (weight, HBM), (down, VMEM)]
        + [(v, VMEM) for v in [total, u_part, y_part, both_next]]
        + [(v, VMEM) for pair in zip(nears, fars) for v in pair],
        [((tokens, local), BF16, VMEM), ((tokens, 2 * proj), F32, VMEM)],
        [
            pltpu.VMEM((parts - 1, tokens, local), BF16),
            pltpu.VMEM((tokens, rank), BF16),
            pltpu.VMEM((tokens, block), F32),
            pltpu.VMEM((ring, block, local), BF16),
            pltpu.SemaphoreType.DMA((ring,)),
        ],
        [both_reach, below[last]],
        18,
    )

    def meet(info, grad, low_last, signs, *rest):
        given, outs, (x,) = dict(zip(turns, rest)), rest[groups:-1], rest[-1:]
        group, part = info[1], info[2]

        @pl.when(info[0] == last)
        def _():
            for k in range(groups):
                origin = group ^ k
                there = pl.ds(pl.multiple_of(lax.rem(origin, spans) * span, 128), span)
                x[pl.ds(pl.multiple_of(origin // spans * proj, proj), proj), there] = given[k][:proj, :]
                if k < spans:
                    x[2 * proj : 4 * proj, there] = given[k][proj:, :]
            x[4 * proj : 5 * proj, :] = low_last[...]
            x[5 * proj :, :] = signs[...]
            y = nt(grad[...], x[...])
            for s in range(last):
                left, right = (y[:, (2 * s + i) * proj : (2 * s + i + 1) * proj] for i in range(2))
                for k in range(parts):
                    chosen = jnp.where(side_of(target_of(part, k)) == 0, left, right).astype(BF16)
                    outs[s * parts + k][:, :proj] = chosen[:half]
                    outs[s * parts + k][:, proj:] = chosen[half:]

    y_all = launch(
        meet,
        [(info, SMEM)] + [(v, VMEM) for v in [below_grad, below[last], signs] + [reach[k] for k in turns]],
        [((half, 2 * proj), BF16, VMEM)] * (last * parts),
        [pltpu.VMEM((2 * last * proj, local), BF16)],
        room=10,
    )
    y_all = [shift(v, [(last, i // parts)], same, i % parts) for i, v in enumerate(y_all)]
    (feats,) = launch(
        features,
        [(info, SMEM), (lengths, SMEM), (own, VMEM)] + [(x, VMEM) for x in x_all] + [(y, VMEM) for y in y_all],
        [((count, share, proj), F32, VMEM)],
        [pltpu.VMEM((tokens, proj), F32)],
        room=8,
    )
    return feats.reshape(count, 1, share * proj)


def solution(mesh):
    placed = (
        P("dp", None, "tensor"),
        P("dp", "pipe", None, "tensor"),
        P("pipe", "tensor", None),
        P("pipe", "tensor", None),
        P("pipe", None, None),
        P(),
        P(),
        P("dp"),
    )
    return jax.shard_map(
        per_device, mesh=mesh, in_specs=placed, out_specs=P("dp", "pipe", "tensor"), check_vma=False
    )
```

```python
import math

import jax
import jax.numpy as jnp
from jax import lax
from jax.experimental import pallas as pl
from jax.experimental.pallas import tpu as pltpu
from jax.sharding import PartitionSpec as P

ADAPTER_SCALE = 2.0
AXES = ("pipe", "dp", "tensor")
F32 = jnp.float32
BF16 = jnp.bfloat16
SMEM, VMEM, HBM, ANY = pltpu.SMEM, pltpu.VMEM, pltpu.HBM, pl.ANY
ROWS = 16
BEST = lax.Precision.HIGHEST


def nt(left, right, precision=None):
    return lax.dot_general(
        left, right, (((1,), (1,)), ((), ())), precision=precision, preferred_element_type=F32
    )


def nn(left, right, precision=None):
    return jnp.dot(left, right, precision=precision, preferred_element_type=F32)


def placed(array, space):
    return pltpu.with_memory_space_constraint(array, HBM) if space is HBM else array


def launch(body, ins, outs, scratch=(), after=(), room=8):
    count, extra = len(ins), len(after)

    def kernel(*refs):
        body(*refs[:count], *refs[count + extra :])

    return pl.pallas_call(
        kernel,
        in_specs=[pl.BlockSpec(memory_space=space) for _, space in ins]
        + [pl.BlockSpec(memory_space=ANY)] * extra,
        out_specs=[pl.BlockSpec(memory_space=space) for _, _, space in outs],
        out_shape=[
            pltpu.HBM(shape, dtype) if space is HBM else jax.ShapeDtypeStruct(shape, dtype)
            for shape, dtype, space in outs
        ],
        scratch_shapes=list(scratch),
        compiler_params=pltpu.CompilerParams(vmem_limit_bytes=room * 2**20),
        cost_estimate=pl.CostEstimate(flops=0, bytes_accessed=0, transcendentals=0),
    )(*[placed(array, space) for array, space in ins], *after)


def shift(value, routes, to_group, by_tensor):
    groups, parts = lax.axis_size("dp"), lax.axis_size("tensor")

    def place(stage, group, part):
        return (stage * groups + group) * parts + part % parts

    pairs = [
        (place(source, g, k), place(target, to_group(g), k + (by_tensor if not more else more[0])))
        for source, target, *more in routes
        for g in range(groups)
        for k in range(parts)
    ]
    return lax.ppermute(value, AXES, pairs)


def copies(sems, *pairs):
    made = [pltpu.make_async_copy(source, target, sems.at[i]) for i, (source, target) in enumerate(pairs)]
    for copy in made:
        copy.start()
    return made


def finish(made):
    for copy in made:
        copy.wait()


def packed_at(lengths, count):
    starts = [jnp.int32(0)]
    for e in range(count):
        starts.append(starts[-1] + (lengths[e] + ROWS - 1) // ROWS * ROWS)
    return starts


def by_rows(rows, sizes, step):
    least = 0
    for size in sizes:
        pl.when((rows > least) & (rows <= size))(lambda size=size: step(size))
        least = size


def per_device(
    output_gradient,
    acts,
    weights,
    adapter_down_factors,
    adapter_up_factors,
    feature_sign_bits,
    rank_sign_bits,
    lengths,
):
    stages, groups, parts = (lax.axis_size(name) for name in AXES)
    last = stages - 1
    count, seq, local = output_gradient.shape
    tokens = count * seq
    half = tokens // 2
    width = local * parts
    rank = adapter_up_factors.shape[1]
    proj = feature_sign_bits.shape[1]
    share = 2 * proj // parts
    near_rows = tokens - proj
    block = min(512, local)
    assert stages == 4 and groups == 4 and parts % 2 == 0 and local % block == 0 and seq % ROWS == 0
    spans = groups // 2
    span = local // spans
    piece = min(512, span)
    per_span = span // piece
    weight, down, up = weights[0], adapter_down_factors[0], adapter_up_factors[0]
    bits = feature_sign_bits.T
    info = jnp.stack([lax.axis_index(name) for name in AXES]).astype(jnp.int32)

    def target_of(part, k):
        return lax.rem(part + k, parts)

    def origin_of(group, k):
        return lax.rem(lax.rem(group, spans) + spans - k, spans)

    def neighbour(k):
        return lambda g: g // spans * spans + (g + k) % spans

    def across(k):
        return lambda g: g ^ k

    def same(g):
        return g

    def columns(which):
        return pl.ds(pl.multiple_of(which * local, 128), local)

    def side_of(part):
        return part // (parts // 2)

    def signs_of(values):
        return (2 * values - 1).astype(F32)

    def prepare(info, bits, low_bits, up, grad, signs, up_low, near, side, low_buf, bits_buf, up_buf, sems):
        mine = columns(info[2])
        made = copies(sems, (low_bits, low_buf), (up.at[:, mine], up_buf), (bits.at[:, mine], bits_buf))
        near_copy = pltpu.make_async_copy(grad.at[:near_rows], near, sems.at[3])
        far_copy = pltpu.make_async_copy(grad.at[near_rows:], side, sems.at[4])
        pl.when(info[0] == last)(near_copy.start)
        pl.when(info[0] == 0)(far_copy.start)
        made[0].wait()
        low_left = signs_of(low_buf[...]).T[:proj, :].astype(BF16)
        made[1].wait()
        up_low[...] = nn(low_left, up_buf[...]).astype(BF16)

        @pl.when(info[0] != 0)
        def _():
            side[...] = up_low[...]

        made[2].wait()
        signs[...] = signs_of(bits_buf[...]).astype(BF16)
        pl.when(info[0] == last)(near_copy.wait)
        pl.when(info[0] == 0)(far_copy.wait)

    def pack(lengths, near, far, target):
        starts = packed_at(lengths, count)
        for e in range(count):
            first, end = e * seq, (e + 1) * seq
            for source, begin, low, high in ((near, 0, first, min(end, near_rows)), (far, near_rows, max(first, near_rows), end)):
                if low < high:
                    there = pl.ds(pl.multiple_of(starts[e] + (low - first), ROWS), high - low)
                    target[there, :] = source[low - begin : high - begin, :]

    near_targets, far_targets = list(range(max(1, parts // 2))), list(range(max(1, parts // 2), parts))
    slots = 3
    far_count, near_count = len(far_targets) * per_span, len(near_targets) * per_span

    order = far_targets + near_targets

    def fetches(info, weight, buffer, sems, first, end):
        made = []
        for i in range(first, end):
            column = (
                target_of(info[2], order[i // per_span]) * local
                + lax.rem(info[1], spans) * span
                + i % per_span * piece
            )
            where = pl.ds(pl.multiple_of(column, 128), piece)
            slot = (i - first) % buffer.shape[0]
            made.append(pltpu.make_async_copy(weight.at[:, where], buffer.at[slot], sems.at[slot]))
        return made

    def lookups(info, up, up_buf, sems, targets):
        pairs = []
        for i, k in enumerate(targets):
            column = target_of(info[2], k) * local + lax.rem(info[1], spans) * span
            pairs.append((up.at[:, pl.ds(pl.multiple_of(column, 128), span)], up_buf.at[i]))
        return copies(sems, *pairs)

    def in_turn(made, ahead, use):
        for copy in made[:ahead]:
            copy.start()
        for i, copy in enumerate(made):
            copy.wait()
            if i + ahead < len(made):
                made[i + ahead].start()
            use(i)

    def first_step(info, weight, down, up, even, signs, *rest):
        outs, (held, x, low, down_buf, up_buf, sems, up_sems) = rest[:parts], rest[parts:]
        stage, group = info[0], info[1]

        @pl.when(stage == 1)
        def _():
            made = fetches(info, weight, held, sems, 0, far_count + near_count)
            ready = lookups(info, up, up_buf, up_sems, order)
            down_copy = pltpu.make_async_copy(down, down_buf, up_sems.at[parts])
            down_copy.start()
            x[...] = jnp.where(group < spans, even[...], signs[...])

            def use(i):
                if i == 0:
                    down_copy.wait()
                    low[...] = (ADAPTER_SCALE * nn(x[...], down_buf[...])).astype(BF16)
                    finish(ready)
                at = pl.ds(i % per_span * piece, piece)
                total = nn(x[...], held[i % far_count]) + nn(low[...], up_buf[i // per_span, :, at])
                outs[order[i // per_span]][:, at] = total.astype(BF16)

            in_turn(made, min(slots, far_count - 1), use)

        @pl.when(stage == 2)
        def _():
            in_turn(fetches(info, weight, held, sems, 0, far_count), far_count, lambda i: None)

    wide = 3 * proj

    def second_far(info, held, down, up, *rest):
        given, rest = rest[: spans * parts + 2], rest[spans * parts + 2 :]
        outs, (x, low, down_buf, up_buf, up_sems) = rest[: len(far_targets)], rest[len(far_targets) :]
        group = info[1]

        @pl.when(info[0] == 2)
        def _():
            ready = lookups(info, up, up_buf, up_sems, far_targets)
            down_copy = pltpu.make_async_copy(down, down_buf, up_sems.at[len(far_targets)])
            down_copy.start()
            for k in range(spans):
                total = given[k * parts][...].astype(F32)
                for value in given[k * parts + 1 : (k + 1) * parts]:
                    total += value[...].astype(F32)
                first = pl.multiple_of(origin_of(group, k) * span, 128)
                x[:proj, pl.ds(first, span)] = total.astype(BF16)
            x[proj : 2 * proj, :] = given[-2][...]
            x[2 * proj :, :] = given[-1][...]
            down_copy.wait()
            low[...] = (ADAPTER_SCALE * nn(x[...], down_buf[...])).astype(BF16)
            finish(ready)
            for i in range(len(far_targets) * per_span):
                at = pl.ds(i % per_span * piece, piece)
                total = nn(x[...], held[i]) + nn(low[...], up_buf[i // per_span, :, at])
                outs[i // per_span][:, at] = total.astype(BF16)

    def second_near(info, weight, up, x, low, *rest):
        outs, (w, up_buf, sems, up_sems) = rest[: len(near_targets)], rest[len(near_targets) :]

        @pl.when(info[0] == 2)
        def _():
            made = fetches(info, weight, w, sems, far_count, far_count + near_count)
            ready = lookups(info, up, up_buf, up_sems, near_targets)

            def use(i):
                if i == 0:
                    finish(ready)
                at = pl.ds(i % per_span * piece, piece)
                total = nn(x[...], w[i % slots]) + nn(low[...], up_buf[i // per_span, :, at])
                outs[i // per_span][:, at] = total.astype(BF16)

            in_turn(made, slots - 1, use)

    def added(values):
        total = values[0].astype(F32)
        for value in values[1:]:
            total += value.astype(F32)
        return total.astype(BF16)

    blocks, ring = local // block, 3

    def stream(weight, ring_buf, sems, count_of, part_of, use):
        def fetch(n):
            i, k = n // count_of, n % count_of
            first = pl.multiple_of(i * block, block)
            slot = lax.rem(n, ring)
            return pltpu.make_async_copy(
                weight.at[pl.ds(first, block), columns(part_of(k))], ring_buf.at[slot], sems.at[slot]
            )

        total_steps = blocks * count_of
        for n in range(min(ring - 1, total_steps)):
            fetch(jnp.int32(n)).start()

        def step(n, _):
            fetch(n).wait()

            @pl.when(n + ring - 1 < total_steps)
            def _():
                fetch(n + ring - 1).start()

            use(n // count_of, n % count_of, lax.rem(n, ring))
            return 0

        return lambda: lax.fori_loop(0, total_steps, step, 0)

    sizes = range(half, tokens + 1, tokens // 8)

    sizes = range(half, tokens + 1, tokens // 8)

    def push_own(info, lengths, raw, bits, weight, up, signs, total, u_part, y_part, both_next, *rest):
        grad, bits_buf, both, ring_buf, sems, ring_sems, tile_sems = rest
        part = info[2]

        @pl.when(info[0] == last)
        def _():
            rows = packed_at(lengths, count)[count]

            def use(i, k, slot):
                at = pl.ds(pl.multiple_of(i * block, block), block)

                def sized(size):
                    total[:size, at] = nt(grad[:size], ring_buf[slot])

                by_rows(rows, sizes, sized)

            starts = packed_at(lengths, count)
            tiles = []
            for e in range(count):
                for j in range(seq // ROWS):
                    there = pl.ds(pl.multiple_of(starts[e] + ROWS * j, ROWS), ROWS)
                    here = pl.ds(e * seq + ROWS * j, ROWS)
                    copy = pltpu.make_async_copy(raw.at[here], grad.at[there], tile_sems.at[len(tiles)])
                    tiles.append((ROWS * j < lengths[e], copy))
            for real, copy in tiles:
                pl.when(real)(copy.start)
            pairs = [(up.at[:, columns(part)], both.at[:rank])]
            for k in range(parts - 1):
                there = columns(target_of(part, k + 1))
                pairs += [(up.at[:, there], both_next.at[k, :rank]), (bits.at[:, there], bits_buf.at[k])]
            made = copies(sems, *pairs)
            go = stream(weight, ring_buf, ring_sems, 1, lambda k: part, use)
            both[rank:, :] = signs[...]
            finish(made)
            for real, copy in tiles:
                pl.when(real)(copy.wait)
            for k in range(parts - 1):
                both_next[k, rank:, :] = signs_of(bits_buf[k]).astype(BF16)
            low = nt(grad[...], both[...])
            u_part[...], y_part[...] = low[:, :rank], low[:, rank:]
            go()

    def push_rest(info, lengths, low_bits, weight, down, total, u_part, y_part, both_next, *rest):
        given, rest = rest[: 2 * (parts - 1)], rest[2 * (parts - 1) :]
        below, own, grad, u_all, so_far, ring_buf, ring_sems = rest
        part = info[2]

        @pl.when(info[0] == last)
        def _():
            rows = packed_at(lengths, count)[count]

            def use(i, k, slot):
                at = pl.ds(pl.multiple_of(i * block, block), block)

                def sized(size):
                    for j in range(parts - 1):

                        @pl.when(k == j)
                        def _(j=j):
                            value = nt(grad[j, :size], ring_buf[slot])
                            if j == 0:
                                value += total[:size, at]
                                value += ADAPTER_SCALE * nt(u_all[:size], down[at, :])
                            else:
                                value += so_far[:size]
                            if j == parts - 2:
                                below[:size, at] = value.astype(BF16)
                            else:
                                so_far[:size] = value

                by_rows(rows, sizes, sized)

            go = stream(weight, ring_buf, ring_sems, parts - 1, lambda k: lax.rem(part + k + 1, parts), use)
            u_sum, y_sum = u_part[...], y_part[...]
            for k in range(parts - 1):
                pack(lengths, given[2 * k], given[2 * k + 1], grad.at[k])
                low = nt(grad[k], both_next[k])
                u_sum += low[:, :rank]
                y_sum += low[:, rank:]
            u_all[...] = u_sum.astype(BF16)
            low_left = signs_of(low_bits[...]).T[:proj, :].astype(BF16)
            own[:, :proj] = nt(u_all[...], low_left)
            own[:, proj:] = y_sum
            go()

    def inputs_side(info, saved, signs, down, low_bits, *rest):
        outs, (saved_buf, down_buf, low_buf, right, both, sems) = rest[:parts], rest[parts:]
        made = copies(sems, (low_bits, low_buf), (down, down_buf), (saved, saved_buf))
        right[:proj, :] = signs[...]
        finish(made[:2])
        turned = nt(signs_of(low_buf[...]).T[proj:, :].astype(BF16), down_buf[...])
        rounded = turned.astype(BF16)
        right[proj : 2 * proj, :] = rounded
        right[2 * proj :, :] = (turned - rounded.astype(F32)).astype(BF16)
        made[2].wait()
        total = nt(right[...], saved_buf[...])
        both[:proj, :] = total[:proj]
        both[proj:, :] = total[proj : 2 * proj] + total[2 * proj :]
        for k in range(parts):
            first = pl.multiple_of(target_of(info[2], k) * share, share)
            outs[k][...] = both[pl.ds(first, share), :]

    scale = ADAPTER_SCALE / math.sqrt(seq) / math.sqrt(width) / math.sqrt(rank)

    def features(info, lengths, own, *rest):
        xs, ys, (out, y) = rest[:parts], rest[parts : (last + 1) * parts], rest[(last + 1) * parts :]
        total = ys[0][...].astype(F32)
        for value in ys[1:]:
            total += value[...].astype(F32)
        y[:half, :] = total[:, :proj]
        y[half:, :] = total[:, proj:]

        @pl.when(info[0] == last)
        def _():
            left = side_of(info[2]) == 0
            y[...] = jnp.where(left, own[:, :proj], own[:, proj:])

        x = xs[0][...]
        for value in xs[1:]:
            x += value[...]
        starts = packed_at(lengths, count)
        for e in range(count):
            real = lengths[e]
            left = x[:, e * seq : (e + 1) * seq] * scale
            left = jnp.where(lax.broadcasted_iota(jnp.int32, left.shape, 1) < real, left, 0.0)
            right = y[pl.ds(pl.multiple_of(starts[e], ROWS), seq), :]
            right = jnp.where(lax.broadcasted_iota(jnp.int32, right.shape, 0) < real, right, 0.0)
            out[e] = nn(left, right, BEST)

    grad = output_gradient.reshape(tokens, local)
    signs, up_low, near, side = launch(
        prepare,
        [(info, SMEM), (bits, HBM), (rank_sign_bits, HBM), (up, HBM), (grad, HBM)],
        [((proj, local), BF16, VMEM)] * 2
        + [((near_rows, local), BF16, VMEM), ((proj, local), BF16, VMEM)],
        [
            pltpu.VMEM(rank_sign_bits.shape, jnp.int32),
            pltpu.VMEM((proj, local), jnp.int32),
            pltpu.VMEM((rank, local), BF16),
            pltpu.SemaphoreType.DMA((5,)),
        ],
        room=8,
    )
    below = [None, shift(up_low, [(0, 1)], same, 0), None, None]
    nears = [shift(near, [(last, last)], same, -k) for k in range(1, parts)]
    fars = [shift(side, [(0, last, -k)] + ([(1, 2, 0)] if k == 1 else []), same, 0) for k in range(1, parts)]
    below[2] = fars[0]
    below[last] = shift(up_low, [(2, last)], same, 0)
    total, u_part, y_part, both_next = launch(
        push_own,
        [(info, SMEM), (lengths, SMEM), (grad, HBM), (bits, HBM), (weight, HBM), (up, HBM), (signs, VMEM)],
        [((tokens, local), F32, VMEM), ((tokens, rank), F32, VMEM), ((tokens, proj), F32, VMEM)]
        + [((parts - 1, rank + proj, local), BF16, VMEM)],
        [
            pltpu.VMEM((tokens, local), BF16),
            pltpu.VMEM((parts - 1, proj, local), jnp.int32),
            pltpu.VMEM((rank + proj, local), BF16),
            pltpu.VMEM((ring, block, local), BF16),
            pltpu.SemaphoreType.DMA((2 * parts,)),
            pltpu.SemaphoreType.DMA((ring,)),
            pltpu.SemaphoreType.DMA((tokens // ROWS,)),
        ],
        room=21,
    )
    *outs, held = launch(
        first_step,
        [(info, SMEM), (weight, HBM), (down, HBM), (up, HBM), (below[1], VMEM), (signs, VMEM)],
        [((proj, span), BF16, VMEM)] * parts + [((far_count, local, piece), BF16, VMEM)],
        [
            pltpu.VMEM((proj, local), BF16),
            pltpu.VMEM((proj, rank), BF16),
            pltpu.VMEM((local, rank), BF16),
            pltpu.VMEM((parts, rank, span), BF16),
            pltpu.SemaphoreType.DMA((far_count,)),
            pltpu.SemaphoreType.DMA((parts + 1,)),
        ],
        [u_part],
        9,
    )
    arrived = [shift(v, [(1, 2)], neighbour(z), k) for z in range(spans) for k, v in enumerate(outs)]
    x_all = launch(
        inputs_side,
        [
            (info, SMEM),
            (acts[:, 0].reshape(tokens, local), HBM),
            (signs, VMEM),
            (down, HBM),
            (rank_sign_bits, HBM),
        ],
        [((share, tokens), F32, VMEM)] * parts,
        [
            pltpu.VMEM((tokens, local), BF16),
            pltpu.VMEM((local, rank), BF16),
            pltpu.VMEM(rank_sign_bits.shape, jnp.int32),
            pltpu.VMEM((3 * proj, local), BF16),
            pltpu.VMEM((2 * proj, tokens), F32),
            pltpu.SemaphoreType.DMA((3,)),
        ],
        [outs[0]],
        12,
    )
    x_all = [
        lax.ppermute(v, "tensor", [(q, (q + k) % parts) for q in range(parts)]) if k else v
        for k, v in enumerate(x_all)
    ]
    *far_outs, x, low = launch(
        second_far,
        [(info, SMEM), (held, VMEM), (down, HBM), (up, HBM)]
        + [(v, VMEM) for v in arrived + [below[2], signs]],
        [((wide, span), BF16, VMEM)] * len(far_targets)
        + [((wide, local), BF16, VMEM), ((wide, rank), BF16, VMEM)],
        [
            pltpu.VMEM((local, rank), BF16),
            pltpu.VMEM((len(far_targets), rank, span), BF16),
            pltpu.SemaphoreType.DMA((len(far_targets) + 1,)),
        ],
        [x_all[0]],
        12,
    )
    near_outs = launch(
        second_near,
        [(info, SMEM), (weight, HBM), (up, HBM), (x, VMEM), (low, VMEM)],
        [((wide, span), BF16, VMEM)] * len(near_targets),
        [
            pltpu.VMEM((slots, local, piece), BF16),
            pltpu.VMEM((len(near_targets), rank, span), BF16),
            pltpu.SemaphoreType.DMA((slots,)),
            pltpu.SemaphoreType.DMA((len(near_targets),)),
        ],
        [far_outs[0]],
        17,
    )
    outs = list(near_outs) + list(far_outs)
    both_reach = added([shift(v, [(2, 2)], same, k) if k else v for k, v in enumerate(outs)])
    turns = list(range(2, groups)) + [1, 0]
    reach = [shift(both_reach[:proj] if k >= spans else both_reach, [(2, last)], across(k), 0) for k in range(groups)]
    below_grad, own = launch(
        push_rest,
        [(info, SMEM), (lengths, SMEM), (rank_sign_bits, VMEM), (weight, HBM), (down, VMEM)]
        + [(v, VMEM) for v in [total, u_part, y_part, both_next]]
        + [(v, VMEM) for pair in zip(nears, fars) for v in pair],
        [((tokens, local), BF16, VMEM), ((tokens, 2 * proj), F32, VMEM)],
        [
            pltpu.VMEM((parts - 1, tokens, local), BF16),
            pltpu.VMEM((tokens, rank), BF16),
            pltpu.VMEM((tokens if parts > 2 else ROWS, block), F32),
            pltpu.VMEM((ring, block, local), BF16),
            pltpu.SemaphoreType.DMA((ring,)),
        ],
        [both_reach, below[last]],
        21,
    )

    def meet(info, grad, low_last, signs, *rest):
        given, outs, (x,) = dict(zip(turns, rest)), rest[groups:-1], rest[-1:]
        group, part = info[1], info[2]

        @pl.when(info[0] == last)
        def _():
            for k in range(groups):
                origin = group ^ k
                there = pl.ds(pl.multiple_of(lax.rem(origin, spans) * span, 128), span)
                x[pl.ds(pl.multiple_of(origin // spans * proj, proj), proj), there] = given[k][:proj, :]
                if k < spans:
                    x[2 * proj : 4 * proj, there] = given[k][proj:, :]
            x[4 * proj : 5 * proj, :] = low_last[...]
            x[5 * proj :, :] = signs[...]

            y = nt(grad[...], x[...])
            for s in range(last):
                left, right = (y[:, (2 * s + i) * proj : (2 * s + i + 1) * proj] for i in range(2))
                for k in range(parts):
                    chosen = jnp.where(side_of(target_of(part, k)) == 0, left, right).astype(BF16)
                    outs[s * parts + k][:, :proj] = chosen[:half]
                    outs[s * parts + k][:, proj:] = chosen[half:]

    y_all = launch(
        meet,
        [(info, SMEM)] + [(v, VMEM) for v in [below_grad, below[last], signs] + [reach[k] for k in turns]],
        [((half, 2 * proj), BF16, VMEM)] * (last * parts),
        [pltpu.VMEM((2 * last * proj, local), BF16)],
        room=10,
    )
    y_all = [shift(v, [(last, i // parts)], same, i % parts) for i, v in enumerate(y_all)]
    (feats,) = launch(
        features,
        [(info, SMEM), (lengths, SMEM), (own, VMEM)] + [(x, VMEM) for x in x_all] + [(y, VMEM) for y in y_all],
        [((count, share, proj), F32, VMEM)],
        [pltpu.VMEM((tokens, proj), F32)],
        room=8,
    )
    return feats.reshape(count, 1, share * proj)


def solution(mesh):
    placed = (
        P("dp", None, "tensor"),
        P("dp", "pipe", None, "tensor"),
        P("pipe", "tensor", None),
        P("pipe", "tensor", None),
        P("pipe", None, None),
        P(),
        P(),
        P("dp"),
    )
    return jax.shard_map(
        per_device, mesh=mesh, in_specs=placed, out_specs=P("dp", "pipe", "tensor"), check_vma=False
    )
```

```python
import math

import jax
import jax.numpy as jnp
from jax import lax
from jax.experimental import pallas as pl
from jax.experimental.pallas import tpu as pltpu
from jax.sharding import PartitionSpec as P

ADAPTER_SCALE = 2.0
AXES = ("pipe", "dp", "tensor")
F32 = jnp.float32
BF16 = jnp.bfloat16
SMEM, VMEM, HBM, ANY = pltpu.SMEM, pltpu.VMEM, pltpu.HBM, pl.ANY
ROWS = 16
BEST = lax.Precision.HIGHEST


def nt(left, right, precision=None):
    return lax.dot_general(
        left, right, (((1,), (1,)), ((), ())), precision=precision, preferred_element_type=F32
    )


def nn(left, right, precision=None):
    return jnp.dot(left, right, precision=precision, preferred_element_type=F32)


def placed(array, space):
    return pltpu.with_memory_space_constraint(array, HBM) if space is HBM else array


def launch(body, ins, outs, scratch=(), after=(), room=8):
    count, extra = len(ins), len(after)

    def kernel(*refs):
        body(*refs[:count], *refs[count + extra :])

    return pl.pallas_call(
        kernel,
        in_specs=[pl.BlockSpec(memory_space=space) for _, space in ins]
        + [pl.BlockSpec(memory_space=ANY)] * extra,
        out_specs=[pl.BlockSpec(memory_space=space) for _, _, space in outs],
        out_shape=[
            pltpu.HBM(shape, dtype) if space is HBM else jax.ShapeDtypeStruct(shape, dtype)
            for shape, dtype, space in outs
        ],
        scratch_shapes=list(scratch),
        compiler_params=pltpu.CompilerParams(vmem_limit_bytes=room * 2**20),
        cost_estimate=pl.CostEstimate(flops=0, bytes_accessed=0, transcendentals=0),
    )(*[placed(array, space) for array, space in ins], *after)


def shift(value, routes, to_group, by_tensor):
    groups, parts = lax.axis_size("dp"), lax.axis_size("tensor")

    def place(stage, group, part):
        return (stage * groups + group) * parts + part % parts

    pairs = [
        (place(source, g, k), place(target, to_group(g), k + (by_tensor if not more else more[0])))
        for source, target, *more in routes
        for g in range(groups)
        for k in range(parts)
    ]
    return lax.ppermute(value, AXES, pairs)


def copies(sems, *pairs):
    made = [pltpu.make_async_copy(source, target, sems.at[i]) for i, (source, target) in enumerate(pairs)]
    for copy in made:
        copy.start()
    return made


def finish(made):
    for copy in made:
        copy.wait()


def packed_at(lengths, count):
    starts = [jnp.int32(0)]
    for e in range(count):
        starts.append(starts[-1] + (lengths[e] + ROWS - 1) // ROWS * ROWS)
    return starts


def by_rows(rows, sizes, step):
    least = 0
    for size in sizes:
        pl.when((rows > least) & (rows <= size))(lambda size=size: step(size))
        least = size


def per_device(
    output_gradient,
    acts,
    weights,
    adapter_down_factors,
    adapter_up_factors,
    feature_sign_bits,
    rank_sign_bits,
    lengths,
):
    stages, groups, parts = (lax.axis_size(name) for name in AXES)
    last = stages - 1
    count, seq, local = output_gradient.shape
    tokens = count * seq
    half = tokens // 2
    width = local * parts
    rank = adapter_up_factors.shape[1]
    proj = feature_sign_bits.shape[1]
    share = 2 * proj // parts
    near_rows = tokens - proj
    block = min(512, local)
    assert stages == 4 and groups == 4 and parts % 2 == 0 and local % block == 0 and seq % ROWS == 0
    spans = groups // 2
    span = local // spans
    piece = min(512, span)
    per_span = span // piece
    weight, down, up = weights[0], adapter_down_factors[0], adapter_up_factors[0]
    bits = feature_sign_bits.T
    info = jnp.stack([lax.axis_index(name) for name in AXES]).astype(jnp.int32)

    def target_of(part, k):
        return lax.rem(part + k, parts)

    def origin_of(group, k):
        return lax.rem(lax.rem(group, spans) + spans - k, spans)

    def neighbour(k):
        return lambda g: g // spans * spans + (g + k) % spans

    def across(k):
        return lambda g: g ^ k

    def same(g):
        return g

    def columns(which):
        return pl.ds(pl.multiple_of(which * local, 128), local)

    def side_of(part):
        return part // (parts // 2)

    def signs_of(values):
        return (2 * values - 1).astype(F32)

    def prepare(info, bits, low_bits, up, grad, signs, up_low, near, side, low_buf, bits_buf, up_buf, sems):
        mine = columns(info[2])
        made = copies(sems, (low_bits, low_buf), (up.at[:, mine], up_buf), (bits.at[:, mine], bits_buf))
        near_copy = pltpu.make_async_copy(grad.at[:near_rows], near, sems.at[3])
        far_copy = pltpu.make_async_copy(grad.at[near_rows:], side, sems.at[4])
        pl.when(info[0] == last)(near_copy.start)
        pl.when(info[0] == 0)(far_copy.start)
        made[0].wait()
        low_left = signs_of(low_buf[...]).T[:proj, :].astype(BF16)
        made[1].wait()
        up_low[...] = nn(low_left, up_buf[...]).astype(BF16)

        @pl.when(info[0] != 0)
        def _():
            side[...] = up_low[...]

        made[2].wait()
        signs[...] = signs_of(bits_buf[...]).astype(BF16)
        pl.when(info[0] == last)(near_copy.wait)
        pl.when(info[0] == 0)(far_copy.wait)

    def pack(lengths, near, far, target):
        starts = packed_at(lengths, count)
        for e in range(count):
            first, end = e * seq, (e + 1) * seq
            for source, begin, low, high in ((near, 0, first, min(end, near_rows)), (far, near_rows, max(first, near_rows), end)):
                if low < high:
                    there = pl.ds(pl.multiple_of(starts[e] + (low - first), ROWS), high - low)
                    target[there, :] = source[low - begin : high - begin, :]

    near_targets, far_targets = list(range(max(1, parts // 2))), list(range(max(1, parts // 2), parts))
    slots = 3
    far_count, near_count = len(far_targets) * per_span, len(near_targets) * per_span

    order = far_targets + near_targets

    def fetches(info, weight, buffer, sems, first, end):
        made = []
        for i in range(first, end):
            column = (
                target_of(info[2], order[i // per_span]) * local
                + lax.rem(info[1], spans) * span
                + i % per_span * piece
            )
            where = pl.ds(pl.multiple_of(column, 128), piece)
            slot = (i - first) % buffer.shape[0]
            made.append(pltpu.make_async_copy(weight.at[:, where], buffer.at[slot], sems.at[slot]))
        return made

    def lookups(info, up, up_buf, sems, targets):
        pairs = []
        for i, k in enumerate(targets):
            column = target_of(info[2], k) * local + lax.rem(info[1], spans) * span
            pairs.append((up.at[:, pl.ds(pl.multiple_of(column, 128), span)], up_buf.at[i]))
        return copies(sems, *pairs)

    def in_turn(made, ahead, use):
        for copy in made[:ahead]:
            copy.start()
        for i, copy in enumerate(made):
            copy.wait()
            if i + ahead < len(made):
                made[i + ahead].start()
            use(i)

    def first_step(info, weight, down, up, even, signs, *rest):
        outs, (held, x, low, down_buf, up_buf, sems, up_sems) = rest[:parts], rest[parts:]
        stage, group = info[0], info[1]

        @pl.when(stage == 1)
        def _():
            made = fetches(info, weight, held, sems, 0, far_count + near_count)
            ready = lookups(info, up, up_buf, up_sems, order)
            down_copy = pltpu.make_async_copy(down, down_buf, up_sems.at[parts])
            down_copy.start()
            x[...] = jnp.where(group < spans, even[...], signs[...])

            def use(i):
                if i == 0:
                    down_copy.wait()
                    low[...] = (ADAPTER_SCALE * nn(x[...], down_buf[...])).astype(BF16)
                    finish(ready)
                at = pl.ds(i % per_span * piece, piece)
                total = nn(x[...], held[i % far_count]) + nn(low[...], up_buf[i // per_span, :, at])
                outs[order[i // per_span]][:, at] = total.astype(BF16)

            in_turn(made, min(slots, far_count - 1), use)

        @pl.when(stage == 2)
        def _():
            in_turn(fetches(info, weight, held, sems, 0, far_count), far_count, lambda i: None)

    def stream_near(info, weight, w, sems, use):
        made = fetches(info, weight, w, sems, far_count, far_count + near_count)
        in_turn(made, slots - 1, use)

    def second_own(info, held, weight, down, up, below, signs, *rest):
        outs, (x, low, down_buf, up_buf, w, sems, up_sems) = rest[:parts], rest[parts:]

        @pl.when(info[0] == 2)
        def _():
            ready = lookups(info, up, up_buf, up_sems, order)
            down_copy = pltpu.make_async_copy(down, down_buf, up_sems.at[parts])
            down_copy.start()
            x[:proj, :] = below[...]
            x[proj:, :] = signs[...]
            down_copy.wait()
            low[...] = (ADAPTER_SCALE * nn(x[...], down_buf[...])).astype(BF16)
            finish(ready)

            def step(i, w_of):
                at = pl.ds(i % per_span * piece, piece)
                total = nn(x[...], w_of) + nn(low[...], up_buf[i // per_span, :, at])
                outs[order[i // per_span]][:, at] = total.astype(BF16)

            made = fetches(info, weight, w, sems, far_count, far_count + near_count)
            for copy in made[: slots - 1]:
                copy.start()
            for i in range(far_count):
                step(i, held[i])
            for i, copy in enumerate(made):
                copy.wait()
                if i + slots - 1 < len(made):
                    made[i + slots - 1].start()
                step(far_count + i, w[i % slots])

    def second_far(info, held, down, up, *rest):
        given, rest = rest[: spans * parts], rest[spans * parts :]
        outs, (x, low, down_buf, up_buf, up_sems) = rest[: len(far_targets)], rest[len(far_targets) :]
        group = info[1]

        @pl.when(info[0] == 2)
        def _():
            ready = lookups(info, up, up_buf, up_sems, far_targets)
            down_copy = pltpu.make_async_copy(down, down_buf, up_sems.at[len(far_targets)])
            down_copy.start()
            for k in range(spans):
                total = given[k * parts][...].astype(F32)
                for value in given[k * parts + 1 : (k + 1) * parts]:
                    total += value[...].astype(F32)
                first = pl.multiple_of(origin_of(group, k) * span, 128)
                x[:, pl.ds(first, span)] = total.astype(BF16)
            down_copy.wait()
            low[...] = (ADAPTER_SCALE * nn(x[...], down_buf[...])).astype(BF16)
            finish(ready)
            for i in range(far_count):
                at = pl.ds(i % per_span * piece, piece)
                total = nn(x[...], held[i]) + nn(low[...], up_buf[i // per_span, :, at])
                outs[i // per_span][:, at] = total.astype(BF16)

    def second_near(info, weight, up, x, low, *rest):
        outs, (w, up_buf, sems, up_sems) = rest[: len(near_targets)], rest[len(near_targets) :]

        @pl.when(info[0] == 2)
        def _():
            ready = lookups(info, up, up_buf, up_sems, near_targets)

            def use(i):
                if i == 0:
                    finish(ready)
                at = pl.ds(i % per_span * piece, piece)
                total = nn(x[...], w[i % slots]) + nn(low[...], up_buf[i // per_span, :, at])
                outs[i // per_span][:, at] = total.astype(BF16)

            stream_near(info, weight, w, sems, use)

    def join(info, *rest):
        firsts, owns, (first, both) = rest[:parts], rest[parts : 2 * parts], rest[2 * parts :]

        @pl.when(info[0] == 2)
        def _():
            for values, row in ((firsts, 0), (owns, proj)):
                total = values[0][...].astype(F32)
                for value in values[1:]:
                    total += value[...].astype(F32)
                both[row : row + total.shape[0], :] = total.astype(BF16)
            first[...] = both[:proj, :]

    blocks, ring = local // block, 3

    def stream(weight, ring_buf, sems, count_of, part_of, use):
        def fetch(n):
            i, k = n // count_of, n % count_of
            first = pl.multiple_of(i * block, block)
            slot = lax.rem(n, ring)
            return pltpu.make_async_copy(
                weight.at[pl.ds(first, block), columns(part_of(k))], ring_buf.at[slot], sems.at[slot]
            )

        total_steps = blocks * count_of
        for n in range(min(ring - 1, total_steps)):
            fetch(jnp.int32(n)).start()

        def step(n, _):
            fetch(n).wait()

            @pl.when(n + ring - 1 < total_steps)
            def _():
                fetch(n + ring - 1).start()

            use(n // count_of, n % count_of, lax.rem(n, ring))
            return 0

        return lambda: lax.fori_loop(0, total_steps, step, 0)

    sizes = range(half, tokens + 1, tokens // 8)

    sizes = range(half, tokens + 1, tokens // 8)

    def push_own(info, lengths, raw, bits, weight, up, signs, total, u_part, y_part, both_next, *rest):
        grad, bits_buf, both, ring_buf, sems, ring_sems, tile_sems = rest
        part = info[2]

        @pl.when(info[0] == last)
        def _():
            rows = packed_at(lengths, count)[count]

            def use(i, k, slot):
                at = pl.ds(pl.multiple_of(i * block, block), block)

                def sized(size):
                    total[:size, at] = nt(grad[:size], ring_buf[slot])

                by_rows(rows, sizes, sized)

            starts = packed_at(lengths, count)
            tiles = []
            for e in range(count):
                for j in range(seq // ROWS):
                    there = pl.ds(pl.multiple_of(starts[e] + ROWS * j, ROWS), ROWS)
                    here = pl.ds(e * seq + ROWS * j, ROWS)
                    copy = pltpu.make_async_copy(raw.at[here], grad.at[there], tile_sems.at[len(tiles)])
                    tiles.append((ROWS * j < lengths[e], copy))
            for real, copy in tiles:
                pl.when(real)(copy.start)
            pairs = [(up.at[:, columns(part)], both.at[:rank])]
            for k in range(parts - 1):
                there = columns(target_of(part, k + 1))
                pairs += [(up.at[:, there], both_next.at[k, :rank]), (bits.at[:, there], bits_buf.at[k])]
            made = copies(sems, *pairs)
            go = stream(weight, ring_buf, ring_sems, 1, lambda k: part, use)
            both[rank:, :] = signs[...]
            finish(made)
            for real, copy in tiles:
                pl.when(real)(copy.wait)
            for k in range(parts - 1):
                both_next[k, rank:, :] = signs_of(bits_buf[k]).astype(BF16)
            low = nt(grad[...], both[...])
            u_part[...], y_part[...] = low[:, :rank], low[:, rank:]
            go()

    def push_rest(info, lengths, low_bits, weight, down, total, u_part, y_part, both_next, *rest):
        given, rest = rest[: 2 * (parts - 1)], rest[2 * (parts - 1) :]
        below, own, grad, u_all, so_far, ring_buf, ring_sems = rest
        part = info[2]

        @pl.when(info[0] == last)
        def _():
            rows = packed_at(lengths, count)[count]

            def use(i, k, slot):
                at = pl.ds(pl.multiple_of(i * block, block), block)

                def sized(size):
                    for j in range(parts - 1):

                        @pl.when(k == j)
                        def _(j=j):
                            value = nt(grad[j, :size], ring_buf[slot])
                            if j == 0:
                                value += total[:size, at]
                                value += ADAPTER_SCALE * nt(u_all[:size], down[at, :])
                            else:
                                value += so_far[:size]
                            if j == parts - 2:
                                below[:size, at] = value.astype(BF16)
                            else:
                                so_far[:size] = value

                by_rows(rows, sizes, sized)

            go = stream(weight, ring_buf, ring_sems, parts - 1, lambda k: lax.rem(part + k + 1, parts), use)
            u_sum, y_sum = u_part[...], y_part[...]
            for k in range(parts - 1):
                pack(lengths, given[2 * k], given[2 * k + 1], grad.at[k])
                low = nt(grad[k], both_next[k])
                u_sum += low[:, :rank]
                y_sum += low[:, rank:]
            u_all[...] = u_sum.astype(BF16)
            low_left = signs_of(low_bits[...]).T[:proj, :].astype(BF16)
            own[:, :proj] = nt(u_all[...], low_left)
            own[:, proj:] = y_sum
            go()

    def inputs_of(info, saved, signs, down, low_bits, rest):
        outs, (saved_buf, down_buf, low_buf, right, both, sems) = rest[:parts], rest[parts:]
        made = copies(sems, (low_bits, low_buf), (down, down_buf), (saved, saved_buf))
        right[:proj, :] = signs[...]
        finish(made[:2])
        turned = nt(signs_of(low_buf[...]).T[proj:, :].astype(BF16), down_buf[...])
        rounded = turned.astype(BF16)
        right[proj : 2 * proj, :] = rounded
        right[2 * proj :, :] = (turned - rounded.astype(F32)).astype(BF16)
        made[2].wait()
        total = nt(right[...], saved_buf[...])
        both[:proj, :] = total[:proj]
        both[proj:, :] = total[proj : 2 * proj] + total[2 * proj :]
        for k in range(parts):
            first = pl.multiple_of(target_of(info[2], k) * share, share)
            outs[k][...] = both[pl.ds(first, share), :]

    def inputs_early(info, saved, signs, down, low_bits, *rest):
        pl.when(info[0] % 2 == 0)(lambda: inputs_of(info, saved, signs, down, low_bits, rest))

    def inputs_late(info, saved, signs, down, low_bits, *rest):
        earlier, rest = rest[:parts], rest[parts:]

        @pl.when(info[0] % 2 == 0)
        def _():
            for value, out in zip(earlier, rest):
                out[...] = value[...]

        pl.when(info[0] % 2 == 1)(lambda: inputs_of(info, saved, signs, down, low_bits, rest))

    scale = ADAPTER_SCALE / math.sqrt(seq) / math.sqrt(width) / math.sqrt(rank)

    def features(info, lengths, own, *rest):
        xs, ys, (out, y) = rest[:parts], rest[parts : (last + 1) * parts], rest[(last + 1) * parts :]
        total = ys[0][...].astype(F32)
        for value in ys[1:]:
            total += value[...].astype(F32)
        y[:half, :] = total[:, :proj]
        y[half:, :] = total[:, proj:]

        @pl.when(info[0] == last)
        def _():
            left = side_of(info[2]) == 0
            y[...] = jnp.where(left, own[:, :proj], own[:, proj:])

        x = xs[0][...]
        for value in xs[1:]:
            x += value[...]
        starts = packed_at(lengths, count)
        for e in range(count):
            real = lengths[e]
            left = x[:, e * seq : (e + 1) * seq] * scale
            left = jnp.where(lax.broadcasted_iota(jnp.int32, left.shape, 1) < real, left, 0.0)
            right = y[pl.ds(pl.multiple_of(starts[e], ROWS), seq), :]
            right = jnp.where(lax.broadcasted_iota(jnp.int32, right.shape, 0) < real, right, 0.0)
            out[e] = nn(left, right, BEST)

    grad = output_gradient.reshape(tokens, local)
    signs, up_low, near, side = launch(
        prepare,
        [(info, SMEM), (bits, HBM), (rank_sign_bits, HBM), (up, HBM), (grad, HBM)],
        [((proj, local), BF16, VMEM)] * 2
        + [((near_rows, local), BF16, VMEM), ((proj, local), BF16, VMEM)],
        [
            pltpu.VMEM(rank_sign_bits.shape, jnp.int32),
            pltpu.VMEM((proj, local), jnp.int32),
            pltpu.VMEM((rank, local), BF16),
            pltpu.SemaphoreType.DMA((5,)),
        ],
        room=8,
    )
    below = [None, shift(up_low, [(0, 1)], same, 0), None, None]
    nears = [shift(near, [(last, last)], same, -k) for k in range(1, parts)]
    fars = [shift(side, [(0, last, -k)] + ([(1, 2, 0)] if k == 1 else []), same, 0) for k in range(1, parts)]
    below[2] = fars[0]
    below[last] = shift(up_low, [(2, last)], same, 0)
    total, u_part, y_part, both_next = launch(
        push_own,
        [(info, SMEM), (lengths, SMEM), (grad, HBM), (bits, HBM), (weight, HBM), (up, HBM), (signs, VMEM)],
        [((tokens, local), F32, VMEM), ((tokens, rank), F32, VMEM), ((tokens, proj), F32, VMEM)]
        + [((parts - 1, rank + proj, local), BF16, VMEM)],
        [
            pltpu.VMEM((tokens, local), BF16),
            pltpu.VMEM((parts - 1, proj, local), jnp.int32),
            pltpu.VMEM((rank + proj, local), BF16),
            pltpu.VMEM((ring, block, local), BF16),
            pltpu.SemaphoreType.DMA((2 * parts,)),
            pltpu.SemaphoreType.DMA((ring,)),
            pltpu.SemaphoreType.DMA((tokens // ROWS,)),
        ],
        room=21,
    )
    def inputs_call(body, given, after):
        return launch(
            body,
            [(info, SMEM), (acts[:, 0].reshape(tokens, local), HBM), (signs, VMEM), (down, HBM), (rank_sign_bits, HBM)]
            + [(v, VMEM) for v in given],
            [((share, tokens), F32, VMEM)] * parts,
            [
                pltpu.VMEM((tokens, local), BF16),
                pltpu.VMEM((local, rank), BF16),
                pltpu.VMEM(rank_sign_bits.shape, jnp.int32),
                pltpu.VMEM((3 * proj, local), BF16),
                pltpu.VMEM((2 * proj, tokens), F32),
                pltpu.SemaphoreType.DMA((3,)),
            ],
            after,
            12,
        )

    x_early = inputs_call(inputs_early, [], [u_part])
    *outs, held = launch(
        first_step,
        [(info, SMEM), (weight, HBM), (down, HBM), (up, HBM), (below[1], VMEM), (signs, VMEM)],
        [((proj, span), BF16, VMEM)] * parts + [((far_count, local, piece), BF16, VMEM)],
        [
            pltpu.VMEM((proj, local), BF16),
            pltpu.VMEM((proj, rank), BF16),
            pltpu.VMEM((local, rank), BF16),
            pltpu.VMEM((parts, rank, span), BF16),
            pltpu.SemaphoreType.DMA((far_count,)),
            pltpu.SemaphoreType.DMA((parts + 1,)),
        ],
        [u_part, x_early[0]],
        9,
    )
    arrived = [shift(v, [(1, 2)], neighbour(z), k) for z in range(spans) for k, v in enumerate(outs)]
    x_all = inputs_call(inputs_late, x_early, [outs[0]])
    owns = launch(
        second_own,
        [(info, SMEM), (held, VMEM), (weight, HBM), (down, HBM), (up, HBM), (below[2], VMEM), (signs, VMEM)],
        [((2 * proj, span), BF16, VMEM)] * parts,
        [
            pltpu.VMEM((2 * proj, local), BF16),
            pltpu.VMEM((2 * proj, rank), BF16),
            pltpu.VMEM((local, rank), BF16),
            pltpu.VMEM((parts, rank, span), BF16),
            pltpu.VMEM((slots, local, piece), BF16),
            pltpu.SemaphoreType.DMA((slots,)),
            pltpu.SemaphoreType.DMA((parts + 1,)),
        ],
        [outs[0]],
        21,
    )
    owns = [shift(v, [(2, 2)], same, k) if k else v for k, v in enumerate(owns)]
    *far_outs, x, low = launch(
        second_far,
        [(info, SMEM), (held, VMEM), (down, HBM), (up, HBM)] + [(v, VMEM) for v in arrived],
        [((proj, span), BF16, VMEM)] * len(far_targets)
        + [((proj, local), BF16, VMEM), ((proj, rank), BF16, VMEM)],
        [
            pltpu.VMEM((local, rank), BF16),
            pltpu.VMEM((len(far_targets), rank, span), BF16),
            pltpu.SemaphoreType.DMA((len(far_targets) + 1,)),
        ],
        [x_all[0]],
        12,
    )
    near_outs = launch(
        second_near,
        [(info, SMEM), (weight, HBM), (up, HBM), (x, VMEM), (low, VMEM)],
        [((proj, span), BF16, VMEM)] * len(near_targets),
        [
            pltpu.VMEM((slots, local, piece), BF16),
            pltpu.VMEM((len(near_targets), rank, span), BF16),
            pltpu.SemaphoreType.DMA((slots,)),
            pltpu.SemaphoreType.DMA((len(near_targets),)),
        ],
        [far_outs[0]],
        17,
    )
    outs = list(near_outs) + list(far_outs)
    firsts = [shift(v, [(2, 2)], same, k) if k else v for k, v in enumerate(outs)]
    first_sum, both_reach = launch(
        join,
        [(info, SMEM)] + [(v, VMEM) for v in firsts + owns],
        [((proj, span), BF16, VMEM), ((3 * proj, span), BF16, VMEM)],
    )
    turns = list(range(2, groups)) + [1, 0]
    reach = [shift(first_sum if k >= spans else both_reach, [(2, last)], across(k), 0) for k in range(groups)]
    below_grad, own = launch(
        push_rest,
        [(info, SMEM), (lengths, SMEM), (rank_sign_bits, VMEM), (weight, HBM), (down, VMEM)]
        + [(v, VMEM) for v in [total, u_part, y_part, both_next]]
        + [(v, VMEM) for pair in zip(nears, fars) for v in pair],
        [((tokens, local), BF16, VMEM), ((tokens, 2 * proj), F32, VMEM)],
        [
            pltpu.VMEM((parts - 1, tokens, local), BF16),
            pltpu.VMEM((tokens, rank), BF16),
            pltpu.VMEM((tokens if parts > 2 else ROWS, block), F32),
            pltpu.VMEM((ring, block, local), BF16),
            pltpu.SemaphoreType.DMA((ring,)),
        ],
        [both_reach, below[last]],
        21,
    )

    def meet(info, grad, low_last, signs, *rest):
        given, outs, (x,) = dict(zip(turns, rest)), rest[groups:-1], rest[-1:]
        group, part = info[1], info[2]

        @pl.when(info[0] == last)
        def _():
            for k in range(groups):
                origin = group ^ k
                there = pl.ds(pl.multiple_of(lax.rem(origin, spans) * span, 128), span)
                x[pl.ds(pl.multiple_of(origin // spans * proj, proj), proj), there] = given[k][:proj, :]
                if k < spans:
                    x[2 * proj : 4 * proj, there] = given[k][proj:, :]
            x[4 * proj : 5 * proj, :] = low_last[...]
            x[5 * proj :, :] = signs[...]

            y = nt(grad[...], x[...])
            for s in range(last):
                left, right = (y[:, (2 * s + i) * proj : (2 * s + i + 1) * proj] for i in range(2))
                for k in range(parts):
                    chosen = jnp.where(side_of(target_of(part, k)) == 0, left, right).astype(BF16)
                    outs[s * parts + k][:, :proj] = chosen[:half]
                    outs[s * parts + k][:, proj:] = chosen[half:]

    y_all = launch(
        meet,
        [(info, SMEM)] + [(v, VMEM) for v in [below_grad, below[last], signs] + [reach[k] for k in turns]],
        [((half, 2 * proj), BF16, VMEM)] * (last * parts),
        [pltpu.VMEM((2 * last * proj, local), BF16)],
        room=10,
    )
    x_all = [
        lax.ppermute(v, "tensor", [(q, (q + k) % parts) for q in range(parts)]) if k else v
        for k, v in enumerate(x_all)
    ]
    y_all = [
        shift(y_all[s * parts + k], [(last, s)], same, k) for s in range(last) for k in reversed(range(parts))
    ]
    (feats,) = launch(
        features,
        [(info, SMEM), (lengths, SMEM), (own, VMEM)] + [(x, VMEM) for x in x_all] + [(y, VMEM) for y in y_all],
        [((count, share, proj), F32, VMEM)],
        [pltpu.VMEM((tokens, proj), F32)],
        room=8,
    )
    return feats.reshape(count, 1, share * proj)


def solution(mesh):
    placed = (
        P("dp", None, "tensor"),
        P("dp", "pipe", None, "tensor"),
        P("pipe", "tensor", None),
        P("pipe", "tensor", None),
        P("pipe", None, None),
        P(),
        P(),
        P("dp"),
    )
    return jax.shard_map(
        per_device, mesh=mesh, in_specs=placed, out_specs=P("dp", "pipe", "tensor"), check_vma=False
    )
```

```python
import math

import jax
import jax.numpy as jnp
from jax import lax
from jax.experimental import pallas as pl
from jax.experimental.pallas import tpu as pltpu
from jax.sharding import PartitionSpec as P

ADAPTER_SCALE = 2.0
AXES = ("pipe", "dp", "tensor")
F32 = jnp.float32
BF16 = jnp.bfloat16
SMEM, VMEM, HBM, ANY = pltpu.SMEM, pltpu.VMEM, pltpu.HBM, pl.ANY
ROWS = 16
BEST = lax.Precision.HIGHEST


def nt(left, right, precision=None):
    return lax.dot_general(
        left, right, (((1,), (1,)), ((), ())), precision=precision, preferred_element_type=F32
    )


def nn(left, right, precision=None):
    return jnp.dot(left, right, precision=precision, preferred_element_type=F32)


def placed(array, space):
    return pltpu.with_memory_space_constraint(array, HBM) if space is HBM else array


def launch(body, ins, outs, scratch=(), after=(), room=8):
    count, extra = len(ins), len(after)

    def kernel(*refs):
        body(*refs[:count], *refs[count + extra :])

    return pl.pallas_call(
        kernel,
        in_specs=[pl.BlockSpec(memory_space=space) for _, space in ins]
        + [pl.BlockSpec(memory_space=ANY)] * extra,
        out_specs=[pl.BlockSpec(memory_space=space) for _, _, space in outs],
        out_shape=[
            pltpu.HBM(shape, dtype) if space is HBM else jax.ShapeDtypeStruct(shape, dtype)
            for shape, dtype, space in outs
        ],
        scratch_shapes=list(scratch),
        compiler_params=pltpu.CompilerParams(vmem_limit_bytes=room * 2**20),
        cost_estimate=pl.CostEstimate(flops=0, bytes_accessed=0, transcendentals=0),
    )(*[placed(array, space) for array, space in ins], *after)


def shift(value, routes, to_group, by_tensor):
    groups, parts = lax.axis_size("dp"), lax.axis_size("tensor")

    def place(stage, group, part):
        return (stage * groups + group) * parts + part % parts

    pairs = [
        (place(source, g, k), place(target, to_group(g), k + (by_tensor if not more else more[0])))
        for source, target, *more in routes
        for g in range(groups)
        for k in range(parts)
    ]
    return lax.ppermute(value, AXES, pairs)


def copies(sems, *pairs):
    made = [pltpu.make_async_copy(source, target, sems.at[i]) for i, (source, target) in enumerate(pairs)]
    for copy in made:
        copy.start()
    return made


def finish(made):
    for copy in made:
        copy.wait()


def packed_at(lengths, count):
    starts = [jnp.int32(0)]
    for e in range(count):
        starts.append(starts[-1] + (lengths[e] + ROWS - 1) // ROWS * ROWS)
    return starts


def by_rows(rows, sizes, step):
    least = 0
    for size in sizes:
        pl.when((rows > least) & (rows <= size))(lambda size=size: step(size))
        least = size


def per_device(
    output_gradient,
    acts,
    weights,
    adapter_down_factors,
    adapter_up_factors,
    feature_sign_bits,
    rank_sign_bits,
    lengths,
):
    stages, groups, parts = (lax.axis_size(name) for name in AXES)
    last = stages - 1
    count, seq, local = output_gradient.shape
    tokens = count * seq
    half = tokens // 2
    width = local * parts
    rank = adapter_up_factors.shape[1]
    proj = feature_sign_bits.shape[1]
    share = 2 * proj // parts
    near_rows = tokens - proj
    block = min(512, local)
    assert stages == 4 and groups == 4 and parts % 2 == 0 and local % block == 0 and seq % ROWS == 0
    spans = groups // 2
    span = local // spans
    piece = min(512, span)
    per_span = span // piece
    weight, down, up = weights[0], adapter_down_factors[0], adapter_up_factors[0]
    bits = feature_sign_bits.T
    info = jnp.stack([lax.axis_index(name) for name in AXES]).astype(jnp.int32)

    def target_of(part, k):
        return lax.rem(part + k, parts)

    def origin_of(group, k):
        return lax.rem(lax.rem(group, spans) + spans - k, spans)

    def neighbour(k):
        return lambda g: g // spans * spans + (g + k) % spans

    def across(k):
        return lambda g: g ^ k

    def same(g):
        return g

    def columns(which):
        return pl.ds(pl.multiple_of(which * local, 128), local)

    def side_of(part):
        return part // (parts // 2)

    def signs_of(values):
        return (2 * values - 1).astype(F32)

    def prepare(info, bits, low_bits, up, grad, signs, up_low, near, side, low_buf, bits_buf, up_buf, sems):
        mine = columns(info[2])
        made = copies(sems, (low_bits, low_buf), (up.at[:, mine], up_buf), (bits.at[:, mine], bits_buf))
        near_copy = pltpu.make_async_copy(grad.at[:near_rows], near, sems.at[3])
        far_copy = pltpu.make_async_copy(grad.at[near_rows:], side, sems.at[4])
        pl.when(info[0] == last)(near_copy.start)
        pl.when(info[0] == 0)(far_copy.start)
        made[0].wait()
        low_left = signs_of(low_buf[...]).T[:proj, :].astype(BF16)
        made[1].wait()
        up_low[...] = nn(low_left, up_buf[...]).astype(BF16)

        @pl.when(info[0] != 0)
        def _():
            side[...] = up_low[...]

        made[2].wait()
        signs[...] = signs_of(bits_buf[...]).astype(BF16)
        pl.when(info[0] == last)(near_copy.wait)
        pl.when(info[0] == 0)(far_copy.wait)

    def pack(lengths, near, far, target):
        starts = packed_at(lengths, count)
        for e in range(count):
            first, end = e * seq, (e + 1) * seq
            for source, begin, low, high in ((near, 0, first, min(end, near_rows)), (far, near_rows, max(first, near_rows), end)):
                if low < high:
                    there = pl.ds(pl.multiple_of(starts[e] + (low - first), ROWS), high - low)
                    target[there, :] = source[low - begin : high - begin, :]

    near_targets, far_targets = list(range(max(1, parts // 2))), list(range(max(1, parts // 2), parts))
    slots = 3
    far_count, near_count = len(far_targets) * per_span, len(near_targets) * per_span

    order = far_targets + near_targets

    def fetches(info, weight, buffer, sems, first, end):
        made = []
        for i in range(first, end):
            column = (
                target_of(info[2], order[i // per_span]) * local
                + lax.rem(info[1], spans) * span
                + i % per_span * piece
            )
            where = pl.ds(pl.multiple_of(column, 128), piece)
            slot = (i - first) % buffer.shape[0]
            made.append(pltpu.make_async_copy(weight.at[:, where], buffer.at[slot], sems.at[slot]))
        return made

    def lookups(info, up, up_buf, sems, targets):
        pairs = []
        for i, k in enumerate(targets):
            column = target_of(info[2], k) * local + lax.rem(info[1], spans) * span
            pairs.append((up.at[:, pl.ds(pl.multiple_of(column, 128), span)], up_buf.at[i]))
        return copies(sems, *pairs)

    def in_turn(made, ahead, use):
        for copy in made[:ahead]:
            copy.start()
        for i, copy in enumerate(made):
            copy.wait()
            if i + ahead < len(made):
                made[i + ahead].start()
            use(i)

    def first_step(info, weight, down, up, even, signs, *rest):
        outs, (held, x, low, down_buf, up_buf, sems, up_sems) = rest[:parts], rest[parts:]
        stage, group = info[0], info[1]

        @pl.when(stage == 1)
        def _():
            made = fetches(info, weight, held, sems, 0, far_count + near_count)
            ready = lookups(info, up, up_buf, up_sems, order)
            down_copy = pltpu.make_async_copy(down, down_buf, up_sems.at[parts])
            down_copy.start()
            x[...] = jnp.where(group < spans, even[...], signs[...])

            def use(i):
                if i == 0:
                    down_copy.wait()
                    low[...] = (ADAPTER_SCALE * nn(x[...], down_buf[...])).astype(BF16)
                    finish(ready)
                at = pl.ds(i % per_span * piece, piece)
                total = nn(x[...], held[i % far_count]) + nn(low[...], up_buf[i // per_span, :, at])
                outs[order[i // per_span]][:, at] = total.astype(BF16)

            in_turn(made, min(slots, far_count - 1), use)

        @pl.when(stage == 2)
        def _():
            in_turn(fetches(info, weight, held, sems, 0, far_count), far_count, lambda i: None)

    wide = 3 * proj

    def second_far(info, held, down, up, *rest):
        given, rest = rest[: spans * parts + 2], rest[spans * parts + 2 :]
        outs, (x, low, down_buf, up_buf, up_sems) = rest[: len(far_targets)], rest[len(far_targets) :]
        group = info[1]

        @pl.when(info[0] == 2)
        def _():
            ready = lookups(info, up, up_buf, up_sems, far_targets)
            down_copy = pltpu.make_async_copy(down, down_buf, up_sems.at[len(far_targets)])
            down_copy.start()
            for k in range(spans):
                total = given[k * parts][...].astype(F32)
                for value in given[k * parts + 1 : (k + 1) * parts]:
                    total += value[...].astype(F32)
                first = pl.multiple_of(origin_of(group, k) * span, 128)
                x[:proj, pl.ds(first, span)] = total.astype(BF16)
            x[proj : 2 * proj, :] = given[-2][...]
            x[2 * proj :, :] = given[-1][...]
            down_copy.wait()
            low[...] = (ADAPTER_SCALE * nn(x[...], down_buf[...])).astype(BF16)
            finish(ready)
            for i in range(len(far_targets) * per_span):
                at = pl.ds(i % per_span * piece, piece)
                total = nn(x[...], held[i]) + nn(low[...], up_buf[i // per_span, :, at])
                outs[i // per_span][:, at] = total.astype(BF16)

    def second_near(info, weight, up, x, low, *rest):
        outs, (w, up_buf, sems, up_sems) = rest[: len(near_targets)], rest[len(near_targets) :]

        @pl.when(info[0] == 2)
        def _():
            made = fetches(info, weight, w, sems, far_count, far_count + near_count)
            ready = lookups(info, up, up_buf, up_sems, near_targets)

            def use(i):
                if i == 0:
                    finish(ready)
                at = pl.ds(i % per_span * piece, piece)
                total = nn(x[...], w[i % slots]) + nn(low[...], up_buf[i // per_span, :, at])
                outs[i // per_span][:, at] = total.astype(BF16)

            in_turn(made, slots - 1, use)

    def added(values):
        total = values[0].astype(F32)
        for value in values[1:]:
            total += value.astype(F32)
        return total.astype(BF16)

    blocks, ring = local // block, 3

    def stream(weight, ring_buf, sems, count_of, part_of, use):
        def fetch(n):
            i, k = n // count_of, n % count_of
            first = pl.multiple_of(i * block, block)
            slot = lax.rem(n, ring)
            return pltpu.make_async_copy(
                weight.at[pl.ds(first, block), columns(part_of(k))], ring_buf.at[slot], sems.at[slot]
            )

        total_steps = blocks * count_of
        for n in range(min(ring - 1, total_steps)):
            fetch(jnp.int32(n)).start()

        def step(n, _):
            fetch(n).wait()

            @pl.when(n + ring - 1 < total_steps)
            def _():
                fetch(n + ring - 1).start()

            use(n // count_of, n % count_of, lax.rem(n, ring))
            return 0

        return lambda: lax.fori_loop(0, total_steps, step, 0)

    sizes = range(half, tokens + 1, tokens // 8)

    sizes = range(half, tokens + 1, tokens // 8)

    def push_own(info, lengths, raw, bits, weight, up, signs, total, u_part, y_part, both_next, *rest):
        grad, bits_buf, both, ring_buf, sems, ring_sems, tile_sems = rest
        part = info[2]

        @pl.when(info[0] == last)
        def _():
            rows = packed_at(lengths, count)[count]

            def use(i, k, slot):
                at = pl.ds(pl.multiple_of(i * block, block), block)

                def sized(size):
                    total[:size, at] = nt(grad[:size], ring_buf[slot])

                by_rows(rows, sizes, sized)

            starts = packed_at(lengths, count)
            tiles = []
            for e in range(count):
                for j in range(seq // ROWS):
                    there = pl.ds(pl.multiple_of(starts[e] + ROWS * j, ROWS), ROWS)
                    here = pl.ds(e * seq + ROWS * j, ROWS)
                    copy = pltpu.make_async_copy(raw.at[here], grad.at[there], tile_sems.at[len(tiles)])
                    tiles.append((ROWS * j < lengths[e], copy))
            for real, copy in tiles:
                pl.when(real)(copy.start)
            pairs = [(up.at[:, columns(part)], both.at[:rank])]
            for k in range(parts - 1):
                there = columns(target_of(part, k + 1))
                pairs += [(up.at[:, there], both_next.at[k, :rank]), (bits.at[:, there], bits_buf.at[k])]
            made = copies(sems, *pairs)
            go = stream(weight, ring_buf, ring_sems, 1, lambda k: part, use)
            both[rank:, :] = signs[...]
            finish(made)
            for real, copy in tiles:
                pl.when(real)(copy.wait)
            for k in range(parts - 1):
                both_next[k, rank:, :] = signs_of(bits_buf[k]).astype(BF16)
            low = nt(grad[...], both[...])
            u_part[...], y_part[...] = low[:, :rank], low[:, rank:]
            go()

    def push_rest(info, lengths, low_bits, weight, down, total, u_part, y_part, both_next, *rest):
        given, rest = rest[: 2 * (parts - 1)], rest[2 * (parts - 1) :]
        below, own, grad, u_all, so_far, ring_buf, ring_sems = rest
        part = info[2]

        @pl.when(info[0] == last)
        def _():
            rows = packed_at(lengths, count)[count]

            def use(i, k, slot):
                at = pl.ds(pl.multiple_of(i * block, block), block)

                def sized(size):
                    for j in range(parts - 1):

                        @pl.when(k == j)
                        def _(j=j):
                            value = nt(grad[j, :size], ring_buf[slot])
                            if j == 0:
                                value += total[:size, at]
                                value += ADAPTER_SCALE * nt(u_all[:size], down[at, :])
                            else:
                                value += so_far[:size]
                            if j == parts - 2:
                                below[:size, at] = value.astype(BF16)
                            else:
                                so_far[:size] = value

                by_rows(rows, sizes, sized)

            go = stream(weight, ring_buf, ring_sems, parts - 1, lambda k: lax.rem(part + k + 1, parts), use)
            u_sum, y_sum = u_part[...], y_part[...]
            for k in range(parts - 1):
                pack(lengths, given[2 * k], given[2 * k + 1], grad.at[k])
                low = nt(grad[k], both_next[k])
                u_sum += low[:, :rank]
                y_sum += low[:, rank:]
            u_all[...] = u_sum.astype(BF16)
            low_left = signs_of(low_bits[...]).T[:proj, :].astype(BF16)
            own[:, :proj] = nt(u_all[...], low_left)
            own[:, proj:] = y_sum
            go()

    def inputs_side(info, saved, signs, down, low_bits, *rest):
        outs, (saved_buf, down_buf, low_buf, right, both, sems) = rest[:parts], rest[parts:]
        made = copies(sems, (low_bits, low_buf), (down, down_buf), (saved, saved_buf))
        right[:proj, :] = signs[...]
        finish(made[:2])
        turned = nt(signs_of(low_buf[...]).T[proj:, :].astype(BF16), down_buf[...])
        rounded = turned.astype(BF16)
        right[proj : 2 * proj, :] = rounded
        right[2 * proj :, :] = (turned - rounded.astype(F32)).astype(BF16)
        made[2].wait()
        total = nt(right[...], saved_buf[...])
        both[:proj, :] = total[:proj]
        both[proj:, :] = total[proj : 2 * proj] + total[2 * proj :]
        for k in range(parts):
            first = pl.multiple_of(target_of(info[2], k) * share, share)
            outs[k][...] = both[pl.ds(first, share), :]

    scale = ADAPTER_SCALE / math.sqrt(seq) / math.sqrt(width) / math.sqrt(rank)

    def features(info, lengths, own, *rest):
        xs, ys, (out, y) = rest[:parts], rest[parts : (last + 1) * parts], rest[(last + 1) * parts :]
        total = ys[0][...].astype(F32)
        for value in ys[1:]:
            total += value[...].astype(F32)
        y[:half, :] = total[:, :proj]
        y[half:, :] = total[:, proj:]

        @pl.when(info[0] == last)
        def _():
            left = side_of(info[2]) == 0
            y[...] = jnp.where(left, own[:, :proj], own[:, proj:])

        x = xs[0][...]
        for value in xs[1:]:
            x += value[...]
        starts = packed_at(lengths, count)
        for e in range(count):
            real = lengths[e]
            left = x[:, e * seq : (e + 1) * seq] * scale
            left = jnp.where(lax.broadcasted_iota(jnp.int32, left.shape, 1) < real, left, 0.0)
            right = y[pl.ds(pl.multiple_of(starts[e], ROWS), seq), :]
            right = jnp.where(lax.broadcasted_iota(jnp.int32, right.shape, 0) < real, right, 0.0)
            out[e] = nn(left, right, BEST)

    grad = output_gradient.reshape(tokens, local)
    signs, up_low, near, side = launch(
        prepare,
        [(info, SMEM), (bits, HBM), (rank_sign_bits, HBM), (up, HBM), (grad, HBM)],
        [((proj, local), BF16, VMEM)] * 2
        + [((near_rows, local), BF16, VMEM), ((proj, local), BF16, VMEM)],
        [
            pltpu.VMEM(rank_sign_bits.shape, jnp.int32),
            pltpu.VMEM((proj, local), jnp.int32),
            pltpu.VMEM((rank, local), BF16),
            pltpu.SemaphoreType.DMA((5,)),
        ],
        room=8,
    )
    below = [None, shift(up_low, [(0, 1)], same, 0), None, None]
    nears = [shift(near, [(last, last)], same, -k) for k in range(1, parts)]
    fars = [shift(side, [(0, last, -k)] + ([(1, 2, 0)] if k == 1 else []), same, 0) for k in range(1, parts)]
    below[2] = fars[0]
    below[last] = shift(up_low, [(2, last)], same, 0)
    total, u_part, y_part, both_next = launch(
        push_own,
        [(info, SMEM), (lengths, SMEM), (grad, HBM), (bits, HBM), (weight, HBM), (up, HBM), (signs, VMEM)],
        [((tokens, local), F32, VMEM), ((tokens, rank), F32, VMEM), ((tokens, proj), F32, VMEM)]
        + [((parts - 1, rank + proj, local), BF16, VMEM)],
        [
            pltpu.VMEM((tokens, local), BF16),
            pltpu.VMEM((parts - 1, proj, local), jnp.int32),
            pltpu.VMEM((rank + proj, local), BF16),
            pltpu.VMEM((ring, block, local), BF16),
            pltpu.SemaphoreType.DMA((2 * parts,)),
            pltpu.SemaphoreType.DMA((ring,)),
            pltpu.SemaphoreType.DMA((tokens // ROWS,)),
        ],
        room=21,
    )
    *outs, held = launch(
        first_step,
        [(info, SMEM), (weight, HBM), (down, HBM), (up, HBM), (below[1], VMEM), (signs, VMEM)],
        [((proj, span), BF16, VMEM)] * parts + [((far_count, local, piece), BF16, VMEM)],
        [
            pltpu.VMEM((proj, local), BF16),
            pltpu.VMEM((proj, rank), BF16),
            pltpu.VMEM((local, rank), BF16),
            pltpu.VMEM((parts, rank, span), BF16),
            pltpu.SemaphoreType.DMA((far_count,)),
            pltpu.SemaphoreType.DMA((parts + 1,)),
        ],
        [u_part],
        9,
    )
    arrived = [shift(v, [(1, 2)], neighbour(z), k) for z in range(spans) for k, v in enumerate(outs)]
    x_all = launch(
        inputs_side,
        [
            (info, SMEM),
            (acts[:, 0].reshape(tokens, local), HBM),
            (signs, VMEM),
            (down, HBM),
            (rank_sign_bits, HBM),
        ],
        [((share, tokens), F32, VMEM)] * parts,
        [
            pltpu.VMEM((tokens, local), BF16),
            pltpu.VMEM((local, rank), BF16),
            pltpu.VMEM(rank_sign_bits.shape, jnp.int32),
            pltpu.VMEM((3 * proj, local), BF16),
            pltpu.VMEM((2 * proj, tokens), F32),
            pltpu.SemaphoreType.DMA((3,)),
        ],
        [outs[0]],
        12,
    )
    x_all = [
        lax.ppermute(v, "tensor", [(q, (q + k) % parts) for q in range(parts)]) if k else v
        for k, v in enumerate(x_all)
    ]
    *far_outs, x, low = launch(
        second_far,
        [(info, SMEM), (held, VMEM), (down, HBM), (up, HBM)]
        + [(v, VMEM) for v in arrived + [below[2], signs]],
        [((wide, span), BF16, VMEM)] * len(far_targets)
        + [((wide, local), BF16, VMEM), ((wide, rank), BF16, VMEM)],
        [
            pltpu.VMEM((local, rank), BF16),
            pltpu.VMEM((len(far_targets), rank, span), BF16),
            pltpu.SemaphoreType.DMA((len(far_targets) + 1,)),
        ],
        [x_all[0]],
        12,
    )
    near_outs = launch(
        second_near,
        [(info, SMEM), (weight, HBM), (up, HBM), (x, VMEM), (low, VMEM)],
        [((wide, span), BF16, VMEM)] * len(near_targets),
        [
            pltpu.VMEM((slots, local, piece), BF16),
            pltpu.VMEM((len(near_targets), rank, span), BF16),
            pltpu.SemaphoreType.DMA((slots,)),
            pltpu.SemaphoreType.DMA((len(near_targets),)),
        ],
        [far_outs[0]],
        17,
    )
    outs = list(near_outs) + list(far_outs)
    both_reach = added([shift(v, [(2, 2)], same, k) if k else v for k, v in enumerate(outs)])
    turns = list(range(2, groups)) + [1, 0]
    reach = [shift(both_reach[:proj] if k >= spans else both_reach, [(2, last)], across(k), 0) for k in range(groups)]
    below_grad, own = launch(
        push_rest,
        [(info, SMEM), (lengths, SMEM), (rank_sign_bits, VMEM), (weight, HBM), (down, VMEM)]
        + [(v, VMEM) for v in [total, u_part, y_part, both_next]]
        + [(v, VMEM) for pair in zip(nears, fars) for v in pair],
        [((tokens, local), BF16, VMEM), ((tokens, 2 * proj), F32, VMEM)],
        [
            pltpu.VMEM((parts - 1, tokens, local), BF16),
            pltpu.VMEM((tokens, rank), BF16),
            pltpu.VMEM((tokens if parts > 2 else ROWS, block), F32),
            pltpu.VMEM((ring, block, local), BF16),
            pltpu.SemaphoreType.DMA((ring,)),
        ],
        [both_reach, below[last]],
        21,
    )

    def meet(info, grad, low_last, signs, *rest):
        given, outs, (x,) = dict(zip(turns, rest)), rest[groups:-1], rest[-1:]
        group, part = info[1], info[2]

        @pl.when(info[0] == last)
        def _():
            for k in range(groups):
                origin = group ^ k
                there = pl.ds(pl.multiple_of(lax.rem(origin, spans) * span, 128), span)
                x[pl.ds(pl.multiple_of(origin // spans * proj, proj), proj), there] = given[k][:proj, :]
                if k < spans:
                    x[2 * proj : 4 * proj, there] = given[k][proj:, :]
            x[4 * proj : 5 * proj, :] = low_last[...]
            x[5 * proj :, :] = signs[...]

            y = nt(grad[...], x[...])
            for s in range(last):
                left, right = (y[:, (2 * s + i) * proj : (2 * s + i + 1) * proj] for i in range(2))
                for k in range(parts):
                    chosen = jnp.where(side_of(target_of(part, k)) == 0, left, right).astype(BF16)
                    outs[s * parts + k][:, :proj] = chosen[:half]
                    outs[s * parts + k][:, proj:] = chosen[half:]

    y_all = launch(
        meet,
        [(info, SMEM)] + [(v, VMEM) for v in [below_grad, below[last], signs] + [reach[k] for k in turns]],
        [((half, 2 * proj), BF16, VMEM)] * (last * parts),
        [pltpu.VMEM((2 * last * proj, local), BF16)],
        room=10,
    )
    y_all = [
        shift(y_all[s * parts + k], [(last, s)], same, k) for s in range(last) for k in reversed(range(parts))
    ]
    (feats,) = launch(
        features,
        [(info, SMEM), (lengths, SMEM), (own, VMEM)] + [(x, VMEM) for x in x_all] + [(y, VMEM) for y in y_all],
        [((count, share, proj), F32, VMEM)],
        [pltpu.VMEM((tokens, proj), F32)],
        room=8,
    )
    return feats.reshape(count, 1, share * proj)


def solution(mesh):
    placed = (
        P("dp", None, "tensor"),
        P("dp", "pipe", None, "tensor"),
        P("pipe", "tensor", None),
        P("pipe", "tensor", None),
        P("pipe", None, None),
        P(),
        P(),
        P("dp"),
    )
    return jax.shard_map(
        per_device, mesh=mesh, in_specs=placed, out_specs=P("dp", "pipe", "tensor"), check_vma=False
    )
```
